32 devices in a mesh: dp: 2 (over x), space: 16 (over z, y, core).
Axes of the slice: x: 2, y: 2, z: 4, core: 2. Of those that a mesh axis runs over, the one named last changes fastest.
Arguments:
- fields: bfloat16 [2, 2048, 100], P('dp', 'space'), may hold values from -6 to 6
- target: bfloat16 [2, 2048, 100], P('dp', 'space'), may hold values from -12 to 12
- area_weight: float32 [2048], P('space'), may hold values from 0.1 to 2.6
- grid_count: int32 [16], P('space'), may hold values from 64 to 128, as said below
- mesh_query: bfloat16 [512, 1024], P('space'), may hold values from -160 to 160
- enc_index: int32 [512, 12], P('space'), may hold values from -1 to 383, as said below
- proc_index: int32 [512, 16], P('space'), may hold values from 0 to 95, as said below
- dec_index: int32 [2048, 3], P('space'), may hold values from 0 to 95, as said below
- w_embed: bfloat16 [100, 1024], P(None, 'dp'), may hold values from -0.625 to 0.625
- w_enc_kv: bfloat16 [1024, 2048], P(None, 'dp'), may hold values from -0.1875 to 0.1875
- w_qkv: bfloat16 [1024, 3072], P(None, 'dp'), may hold values from -0.1875 to 0.1875
- w_out: bfloat16 [1024, 1024], P('dp'), may hold values from -0.1875 to 0.1875
- w_dec1: bfloat16 [1024, 1024], P(None, 'dp'), may hold values from -0.1875 to 0.1875
- w_dec2: bfloat16 [1024, 100], P('dp'), may hold values from -0.1875 to 0.1875
Outputs:
- prediction: bfloat16 [2, 2048, 100], P('dp', 'space')
- loss: float32 [], replicated
The draws below stay inside these ranges and needn't reach their ends.
Inputs may be any that keep to these rules, and one draw needn't show every extreme that they name: The first grid_count slots of a device are real points; some device holds 128 and some other 64. `enc_index`: an entry e >= 0 of mesh node m names slot e mod 128 of device m // 32 - 1 + e // 128, an existing device, and a slot below its grid_count; -1 marks padding, each row has 6 to 12 real entries, first. `proc_index`: an entry e of mesh node m names node e mod 32 of device m // 32 - 1 + e // 32, an existing device; the first entry is the node itself. `dec_index`: an entry e of grid slot g names node e mod 32 of device g // 128 - 1 + e // 32, an existing device.
All inputs are finite; a program needn't handle non-finite values.
Results may differ from the reference program's by a relative error of at most 0.012.
Values may be sent and summed in bfloat16 or wider, within the bound.
No kernel may reach another device: no remote copies, remote signals or barrier semaphores. Data moves between devices by JAX's collectives and lax.ppermute only.
A program may use at most 64 MiB of HBM per device.

```python
import math
import jax
import jax.numpy as jnp
from jax import lax

H = 1024
HEADS = 16
FIELDS = 100
K_ENC = 12
K_DEC = 3
K_PROC = 16
G_DEV = 128
M_DEV = 32
GRID = 2048
MESH = 512
SAMPLES = 2
N_SPACE = 16


def full_and_half(key):
    devices = GRID // G_DEV
    first = jax.random.randint(jax.random.fold_in(key, 12), (), 0, devices - 1)
    second = jax.random.randint(jax.random.fold_in(key, 13), (), 0, devices - 1)
    full_device = 1 + first
    half_device = (full_device + 1 + second) % devices
    return (full_device, half_device)


def device_counts(key):
    devices = GRID // G_DEV
    counts = jax.random.randint(jax.random.fold_in(key, 11), (devices,), G_DEV // 2, G_DEV + 1)
    full_device, half_device = full_and_half(key)
    places = jnp.arange(devices)
    counts = jnp.where(places == full_device, G_DEV, counts)
    counts = jnp.where(places == half_device, G_DEV // 2, counts)
    return counts.astype(jnp.int32)


def row_share(key):
    return jax.random.uniform(jax.random.fold_in(key, 5), (GRID,), jnp.float32, 0.0, 1.0)


def neighbour_sides(key, row_total, per_device, columns):
    devices = GRID // G_DEV
    owner = (jnp.arange(row_total) // per_device)[:, None]
    anchor = jax.random.randint(key, (row_total, columns), 0, 3)
    anchor = jnp.where((owner == 0) & (anchor == 0), 1, anchor)
    anchor = jnp.where((owner == devices - 1) & (anchor == 2), 1, anchor)
    return (owner, anchor)


def draw_grid_count(key, part):
    return device_counts(key)


def draw_enc_index(key, part):
    devices = GRID // G_DEV
    counts = device_counts(key)
    full_device, half_device = full_and_half(key)
    owner, anchor = neighbour_sides(jax.random.fold_in(key, 21), MESH, M_DEV, K_ENC)
    source = jnp.clip(owner - 1 + anchor, 0, devices - 1)
    limits = counts[source]
    slot_index = jax.random.randint(jax.random.fold_in(key, 22), (MESH, K_ENC), 0, limits)
    real_count = jax.random.randint(jax.random.fold_in(key, 23), (MESH, 1), 6, K_ENC + 1)
    rows = jnp.arange(MESH)[:, None]
    real_count = jnp.where(rows == 0, 6, real_count)
    entries = anchor * G_DEV + slot_index
    columns = jnp.arange(K_ENC)[None, :]
    top_row = (full_device - 1) * M_DEV
    entries = jnp.where((rows == top_row) & (columns == 0), 3 * G_DEV - 1, entries)
    return jnp.where(columns < real_count, entries, -1).astype(jnp.int32)


def draw_proc_index(key, part):
    owner, anchor = neighbour_sides(jax.random.fold_in(key, 31), MESH, M_DEV, K_PROC)
    slot_index = jax.random.randint(jax.random.fold_in(key, 32), (MESH, K_PROC), 0, M_DEV)
    entries = anchor * M_DEV + slot_index
    rows = jnp.arange(MESH)[:, None]
    columns = jnp.arange(K_PROC)[None, :]
    entries = jnp.where((rows == 0) & (columns == 1), 3 * M_DEV - 1, entries)
    entries = jnp.where((rows == M_DEV) & (columns == 2), 0, entries)
    itself = (M_DEV + jnp.arange(MESH) % M_DEV)[:, None]
    return jnp.where(columns == 0, itself, entries).astype(jnp.int32)


def draw_dec_index(key, part):
    owner, anchor = neighbour_sides(jax.random.fold_in(key, 41), GRID, G_DEV, K_DEC)
    slot_index = jax.random.randint(jax.random.fold_in(key, 42), (GRID, K_DEC), 0, M_DEV)
    entries = anchor * M_DEV + slot_index
    rows = jnp.arange(GRID)[:, None]
    columns = jnp.arange(K_DEC)[None, :]
    entries = jnp.where((rows == 0) & (columns == 0), 3 * M_DEV - 1, entries)
    entries = jnp.where((rows == G_DEV) & (columns == 0), 0, entries)
    return entries.astype(jnp.int32)


def draw_area_weight(key, part):
    share = row_share(key)
    positions = jnp.arange(GRID).astype(jnp.float32)
    baseline = 0.5 + 1.5 * positions / GRID
    factor = 0.3 + share
    return (baseline * factor).astype(jnp.float32)


def draw_target(key, part):
    share = row_share(key)
    blocks = GRID // G_DEV
    field_scale = jnp.exp(jax.random.uniform(jax.random.fold_in(key, 61), (1, 1, FIELDS), jnp.float32, jnp.log(0.3), jnp.log(1.0)))
    block_table = jnp.exp(jax.random.uniform(jax.random.fold_in(key, 64), (blocks, FIELDS), jnp.float32, jnp.log(0.3), jnp.log(2.0)))
    block_scale = jnp.repeat(block_table, G_DEV, axis=0)[None, :, :]
    row_scale = (0.5 * jnp.exp(jnp.log(6.0) * share))[None, :, None]
    position = jnp.arange(SAMPLES).astype(jnp.float32) / max(SAMPLES - 1, 1)
    sample_scale = (1.0 + position)[:, None, None]
    values = jnp.clip(jax.random.normal(jax.random.fold_in(key, 63), (SAMPLES, GRID, FIELDS), jnp.float32), -4.0, 4.0)
    values = values * field_scale * block_scale * row_scale * sample_scale
    return jnp.clip(values, -12.0, 12.0).astype(jnp.bfloat16)


def draw_mesh_query(key, part):
    values = jnp.clip(jax.random.normal(jax.random.fold_in(key, 71), (MESH, H), jnp.float32), -4.0, 4.0)
    return values.astype(jnp.bfloat16)


def shard_levels(own_key, shape, shards, low, high):
    def one(axis_at, parts):
        heights = jax.random.uniform(jax.random.fold_in(jax.random.fold_in(own_key, 6), axis_at), (parts,), jnp.float32, low / len(shards), high / len(shards))
        return jnp.repeat(jnp.exp(heights), shape[axis_at] // parts).reshape((-1,) + (1,) * (len(shape) - axis_at - 1))

    gain = one(*shards[0])
    for cut in shards[1:]:
        gain = gain * one(*cut)
    return gain


def noise(key, shape, scale, limit, split=(), kind=jnp.bfloat16):
    result = scale * jax.random.normal(key, shape, jnp.float32)
    if split:
        result = result * shard_levels(key, shape, split, -0.22, 0.18)
    return jnp.clip(result, -limit, limit).astype(kind)


def setup_inputs(seed: int = 0) -> dict:
    key_list = jax.random.split(jax.random.key(seed), 15)
    fields = noise(key_list[0], (SAMPLES, GRID, FIELDS), 1.0, 6.0, ((0, 2), (1, 16)))
    target = draw_target(jax.random.fold_in(key_list[14], 71), 0)
    area_weight = draw_area_weight(jax.random.fold_in(key_list[14], 71), 0)
    grid_count = draw_grid_count(jax.random.fold_in(key_list[14], 71), 0)
    mesh_query = draw_mesh_query(jax.random.fold_in(key_list[14], 71), 0)
    enc_index = draw_enc_index(jax.random.fold_in(key_list[14], 71), 0)
    proc_index = draw_proc_index(jax.random.fold_in(key_list[14], 71), 0)
    dec_index = draw_dec_index(jax.random.fold_in(key_list[14], 71), 0)
    w_embed = noise(key_list[8], (FIELDS, H), FIELDS ** -0.5, 0.625, ((1, 2),))
    w_enc_kv = noise(key_list[9], (H, 2 * H), H ** -0.5, 0.1875, ((1, 2),))
    w_qkv = noise(key_list[10], (H, 3 * H), H ** -0.5, 0.1875, ((1, 2),))
    w_out = noise(key_list[11], (H, H), H ** -0.5, 0.1875, ((0, 2),))
    w_dec1 = noise(key_list[12], (H, H), H ** -0.5, 0.1875, ((1, 2),))
    w_dec2 = noise(key_list[13], (H, FIELDS), H ** -0.5, 0.1875, ((0, 2),))
    return dict(fields=fields, target=target, area_weight=area_weight, grid_count=grid_count, mesh_query=mesh_query, enc_index=enc_index, proc_index=proc_index, dec_index=dec_index, w_embed=w_embed, w_enc_kv=w_enc_kv, w_qkv=w_qkv, w_out=w_out, w_dec1=w_dec1, w_dec2=w_dec2)


def layer_norm(values):
    centre = lax.optimization_barrier(jnp.mean(values, axis=-1, keepdims=True))
    shifted = values - centre
    spread = lax.optimization_barrier(jnp.mean(shifted * shifted, axis=-1, keepdims=True))
    return shifted / jnp.sqrt(spread + 1e-05)

def attend(queries, gathered, present):
    node_count, width = queries.shape
    per_head_width = width // HEADS
    split_query_heads = queries.astype(jnp.float32).reshape(node_count, HEADS, per_head_width)
    split_key_heads = gathered[:, :, :width].astype(jnp.float32).reshape(node_count, -1, HEADS, per_head_width)
    split_value_heads = gathered[:, :, width:].astype(jnp.float32).reshape(node_count, -1, HEADS, per_head_width)
    attention_logits = jnp.einsum('gtz,gxtz->gtx', split_query_heads, split_key_heads) / math.sqrt(per_head_width)
    attention_logits = jnp.where(present[:, None, :], attention_logits, -jnp.inf)
    attention_probs = jax.nn.softmax(attention_logits, axis=-1).astype(jnp.bfloat16)
    aggregated_values = jnp.einsum('owi,oiwn->own', attention_probs.astype(jnp.float32), split_value_heads)
    return aggregated_values.reshape(node_count, width)

def reference(fields, target, area_weight, grid_count, mesh_query, enc_index, proc_index, dec_index, w_embed, w_enc_kv, w_qkv, w_out, w_dec1, w_dec2):
    devices = jnp.arange(N_SPACE, dtype=jnp.int32)
    slot_ids = jnp.arange(GRID, dtype=jnp.int32)
    valid = slot_ids % G_DEV < jnp.repeat(grid_count, G_DEV)
    keep_mask = valid.astype(jnp.float32)

    def one_sample(pair):
        sample_fields, sample_target = pair
        embedded = jax.nn.silu(jnp.dot(sample_fields, w_embed, preferred_element_type=jnp.float32)).astype(jnp.bfloat16)
        enc_pairs = jnp.dot(embedded, w_enc_kv, preferred_element_type=jnp.float32).astype(jnp.bfloat16)

        def encode(item):
            queries, neighbours, device = item
            present = neighbours >= 0
            global_ids = jnp.clip(neighbours + (device - 1) * G_DEV, 0, GRID - 1).astype(jnp.int32)
            gathered = jnp.take(enc_pairs, global_ids, axis=0)
            return (queries.astype(jnp.float32) + attend(queries, gathered, present)).astype(jnp.bfloat16)
        latent = lax.map(encode, (mesh_query.reshape(N_SPACE, M_DEV, H), enc_index.reshape(N_SPACE, M_DEV, K_ENC), devices)).reshape(MESH, H)
        normed = layer_norm(latent.astype(jnp.float32)).astype(jnp.bfloat16)
        mesh_qkv = jnp.dot(normed, w_qkv, preferred_element_type=jnp.float32).astype(jnp.bfloat16)
        mesh_pairs = mesh_qkv[:, H:]

        def process(item):
            queries, neighbours, device = item
            global_ids = (neighbours + (device - 1) * M_DEV).astype(jnp.int32)
            gathered = jnp.take(mesh_pairs, global_ids, axis=0)
            return attend(queries, gathered, jnp.ones(neighbours.shape, dtype=bool)).astype(jnp.bfloat16)
        mixed = lax.map(process, (mesh_qkv[:, :H].reshape(N_SPACE, M_DEV, H), proc_index.reshape(N_SPACE, M_DEV, K_PROC), devices)).reshape(MESH, H)
        updated = (latent.astype(jnp.float32) + jnp.dot(mixed, w_out, preferred_element_type=jnp.float32)).astype(jnp.bfloat16)

        def decode(item):
            neighbours, device = item
            global_ids = (neighbours + (device - 1) * M_DEV).astype(jnp.int32)
            nearby = jnp.take(updated, global_ids, axis=0).astype(jnp.float32)
            return layer_norm(lax.optimization_barrier(jnp.mean(nearby, axis=1))).astype(jnp.bfloat16)
        decoder_in = lax.map(decode, (dec_index.reshape(N_SPACE, G_DEV, K_DEC), devices)).reshape(GRID, H)
        decoder_hidden = jax.nn.silu(jnp.dot(decoder_in, w_dec1, preferred_element_type=jnp.float32)).astype(jnp.bfloat16)
        increment = jnp.dot(decoder_hidden, w_dec2, preferred_element_type=jnp.float32)
        predicted = jnp.where(valid[:, None], sample_fields.astype(jnp.float32) + increment, jnp.float32(0.0))
        target_rows = sample_target.astype(jnp.float32)
        misfit = predicted - target_rows
        error_sums = lax.optimization_barrier(jnp.sum((keep_mask * area_weight)[:, None] * misfit * misfit, axis=0))
        target_sums = lax.optimization_barrier(jnp.sum(keep_mask[:, None] * target_rows * target_rows, axis=0))
        return (predicted.astype(jnp.bfloat16), error_sums, target_sums)
    prediction, error_parts, target_parts = lax.map(one_sample, (fields, target))
    valid_count = SAMPLES * jnp.sum(keep_mask)
    weight_sum = SAMPLES * jnp.sum(keep_mask * area_weight)
    scale = lax.optimization_barrier(jnp.sum(target_parts, axis=0)) / valid_count + 1e-05
    loss = jnp.sum(lax.optimization_barrier(jnp.sum(error_parts, axis=0)) / scale) / (FIELDS * weight_sum)
    return (prediction, loss)
```

```python
import functools
import math

import jax
import jax.numpy as jnp
from jax import lax
from jax.experimental import pallas as pl
from jax.experimental.pallas import tpu as pltpu
from jax.sharding import PartitionSpec as P

HEADS = 16
F32 = jnp.float32
BF16 = jnp.bfloat16


def silu(x):
    return 0.5 * x * (1.0 + jnp.tanh(0.5 * x))


def dot(a, b):
    return jnp.dot(a, b, preferred_element_type=F32)


def dot_nt(a, b):
    return lax.dot_general(a, b, (((1,), (1,)), ((), ())), preferred_element_type=F32)


def normalize(values):
    centre = jnp.mean(values, axis=-1, keepdims=True)
    shifted = values - centre
    spread = jnp.mean(shifted * shifted, axis=-1, keepdims=True)
    return shifted * lax.rsqrt(spread + 1e-05)


def call(kernel, out_shape, args, scratch=(), flops=0, smem=(0,)):
    specs = [
        pl.BlockSpec(memory_space=pltpu.SMEM if i in smem else pltpu.VMEM) for i in range(len(args))
    ]
    many = isinstance(out_shape, (list, tuple))
    out_specs = jax.tree.map(lambda _: pl.BlockSpec(memory_space=pltpu.VMEM), out_shape)
    size = sum(math.prod(a.shape) * a.dtype.itemsize for a in args)
    return pl.pallas_call(
        kernel,
        out_shape=out_shape,
        in_specs=specs,
        out_specs=tuple(out_specs) if many else out_specs,
        scratch_shapes=list(scratch),
        compiler_params=pltpu.CompilerParams(vmem_limit_bytes=48 * 1024 * 1024),
        cost_estimate=pl.CostEstimate(flops=flops, bytes_accessed=size, transcendentals=0),
    )(*args)


def encode_kernel(
    place, own, own1, own2, oth, oth1, oth2, pick, present, we_here, we_there, w_ref, query,
    pairs_ref, probs_ref,
):
    half = we_here.shape[1]
    nodes, width = query.shape
    rows = pick.shape[0]
    slots = own.shape[0]
    entries = rows // nodes
    per_head = width // HEADS
    here = pl.multiple_of(place[0] * half, half)
    there = pl.multiple_of((1 - place[0]) * half, half)
    head_of = lax.broadcasted_iota(jnp.int32, (width, 128), 0) // per_head
    fold = (head_of == lax.broadcasted_iota(jnp.int32, (width, 128), 1)).astype(BF16)
    queries = jnp.broadcast_to(query[...].astype(F32)[None], (entries, nodes, width))
    queries = queries.reshape(rows, width)
    there_mask = present[...] > 0
    for s, blocks in enumerate(((own, own1, own2), (oth, oth1, oth2))):
        near = sum(dot(pick[:, i * slots : (i + 1) * slots], b[...]) for i, b in enumerate(blocks))
        near = near.astype(BF16)
        embed_here = silu(dot(near, we_here[...])).astype(BF16)
        embed_there = silu(dot(near, we_there[...])).astype(BF16)
        pairs = dot(embed_here, w_ref[pl.ds(here, half), :])
        pairs = (pairs + dot(embed_there, w_ref[pl.ds(there, half), :])).astype(BF16)
        pairs_ref[s * rows : (s + 1) * rows, :] = pairs
        product = pairs.astype(F32) * queries
        high = product.astype(BF16)
        low = (product - high.astype(F32)).astype(BF16)
        logits = (dot(high, fold) + dot(low, fold)) * (1.0 / math.sqrt(per_head))
        logits = jnp.where(there_mask, logits, -1e30).reshape(entries, nodes, 128)
        top = jnp.max(logits, axis=0, keepdims=True)
        weight = jnp.where(there_mask.reshape(entries, nodes, 128), jnp.exp(logits - top), 0.0)
        weight = weight / jnp.sum(weight, axis=0, keepdims=True)
        turned = jnp.transpose(weight.reshape(rows, 128))
        probs_ref[:, s * rows : (s + 1) * rows] = turned[:HEADS].astype(BF16)


def latent_kernel(probs, pairs, query, latent_ref):
    nodes, width = query.shape
    rows = pairs.shape[0] // 2
    entries = rows // nodes
    per_head = width // HEADS
    head_of = lax.broadcasted_iota(jnp.int32, (HEADS, width), 1) // per_head
    spread = (head_of == lax.broadcasted_iota(jnp.int32, (HEADS, width), 0)).astype(BF16)
    for s in range(2):
        turned = probs[:, (1 - s) * rows : (2 - s) * rows].astype(F32)
        weight = jnp.transpose(turned).astype(BF16)
        mixed = dot(weight, spread) * pairs[s * rows : (s + 1) * rows, :].astype(F32)
        mixed = jnp.sum(mixed.reshape(entries, nodes, width), axis=0)
        latent_ref[s * nodes : (s + 1) * nodes, :] = (query[...].astype(F32) + mixed).astype(BF16)


def mesh_kernel(
    place, lat0, lat1, lat2, count, w_ref, same_ref, cross_ref, wo_ref,
    keep_ref, send_ref, norm_ref,
):
    both, width = lat0.shape
    nodes = both // 2
    half = width // 2
    rows = 3 * both
    heads = HEADS // 2
    per_head = half // heads
    for i, block in enumerate((lat0, lat1, lat2)):
        norm_ref[i * both : (i + 1) * both, :] = normalize(block[...].astype(F32)).astype(BF16)
    here = pl.multiple_of(place[1] * half, half)
    there = pl.multiple_of((1 - place[1]) * half, half)
    first = place[0] == 0
    part_a = dot(norm_ref[...], w_ref[:, :half])
    part_c = dot(norm_ref[...], w_ref[:, 2 * half :])
    part_b = dot(norm_ref[:, pl.ds(here, half)], same_ref[...])
    part_b += dot(norm_ref[:, pl.ds(there, half)], cross_ref[...])
    queries = jnp.where(first, part_a[:both], part_b[:both]).astype(BF16)
    keys = jnp.where(first, part_c, part_a).astype(BF16)
    values = jnp.where(first, part_b, part_c).astype(BF16)
    head_of = lax.broadcasted_iota(jnp.int32, (both, half), 1) // per_head
    zero = jnp.zeros_like(queries)
    stacked = jnp.concatenate(
        [jnp.where(head_of == h, queries, zero) for h in range(heads)], axis=0
    )
    logits = dot_nt(stacked, keys) * (1.0 / math.sqrt(per_head))
    logits = logits.reshape(heads, both, rows)
    times = count[...][None]
    logits = jnp.where(times > 0, logits, -1e30)
    top = jnp.max(logits, axis=-1, keepdims=True)
    weight = times * jnp.exp(logits - top)
    weight = weight / jnp.sum(weight, axis=-1, keepdims=True)
    mixed = dot(weight.astype(BF16).reshape(heads * both, rows), values)
    mixed = mixed.reshape(heads, both, half)
    total = jnp.where(head_of == 0, mixed[0], 0.0)
    for h in range(1, heads):
        total = jnp.where(head_of == h, mixed[h], total)
    projected = dot(total.astype(BF16), wo_ref[...])
    keep_ref[...] = lat0[:nodes, :].astype(F32) + projected[:nodes]
    send_ref[...] = projected[nodes:].astype(BF16)


def decode_kernel(
    place, up0, up1, up2, count, w1_ref, same_ref, cross_ref, w2_ref, w2_there, fields, target,
    area, valid, pred_ref, sums_ref, norm_ref,
):
    nodes, width = up0.shape
    half = width // 2
    near = sum(
        dot(count[:, i * nodes : (i + 1) * nodes], b[...]) for i, b in enumerate((up0, up1, up2))
    )
    norm_ref[...] = normalize(near * (1.0 / 3.0)).astype(BF16)
    here = pl.multiple_of(place[1] * half, half)
    there = pl.multiple_of((1 - place[1]) * half, half)
    hidden = silu(dot(norm_ref[...], w1_ref[...])).astype(BF16)
    hidden_there = dot(norm_ref[:, pl.ds(here, half)], same_ref[...])
    hidden_there += dot(norm_ref[:, pl.ds(there, half)], cross_ref[...])
    hidden_there = silu(hidden_there).astype(BF16)
    increment = dot(hidden, w2_ref[...]) + dot(hidden_there, w2_there[...])
    keep = valid[...] > 0
    predicted = jnp.where(keep, fields[...].astype(F32) + increment, 0.0)
    pred_ref[...] = predicted.astype(BF16)
    goal = target[...].astype(F32)
    misfit = predicted - goal
    weight = jnp.where(keep, area[...], 0.0)
    count_field = fields.shape[1]
    errors = jnp.sum(weight * misfit * misfit, axis=0, keepdims=True)
    squares = jnp.sum(jnp.where(keep, goal * goal, 0.0), axis=0, keepdims=True)
    here_count = jnp.sum(valid[...], axis=0, keepdims=True)
    here_weight = jnp.sum(weight, axis=0, keepdims=True)
    sums = jnp.concatenate(
        [
            errors,
            squares,
            jnp.broadcast_to(here_count, (1, count_field)),
            jnp.broadcast_to(here_weight, (1, count_field)),
            jnp.zeros((4, count_field), F32),
        ],
        axis=0,
    )
    sums_ref[...] = jnp.broadcast_to(sums[None], sums_ref.shape)


def loss_kernel(parts, loss_ref):
    total = jnp.sum(parts[...], axis=0)
    fields = total.shape[1]
    scaled = total[0:1] / (total[1:2] / total[2:3] + 1e-05)
    weight = total[3:4, 0:1]
    loss_ref[...] = jnp.sum(scaled, axis=1, keepdims=True) / (fields * weight)


def small_body(
    fields, target, area_weight, grid_count, mesh_query, enc_index, proc_index, dec_index,
    w_embed, w_enc_kv, w_qkv, w_out, w_dec1, w_dec2,
):
    space = lax.axis_size("space")
    samples = lax.axis_size("dp")
    row = lax.axis_index("dp")
    spot = lax.axis_index("space")
    core = spot % 2
    place = jnp.stack([row, core]).astype(jnp.int32)
    own = fields[0]
    slots, field_count = own.shape
    nodes, width = mesh_query.shape
    half = width // 2
    entries = enc_index.shape[1]
    rows = nodes * entries

    swap = [(0, 1), (1, 0)]
    pair = [(i, i ^ 1) for i in range(space)]
    link = [(i, i + 1) for i in range(1, space - 1, 2)]
    link = link + [(j, i) for i, j in link]
    cross = [(d * space + i, (1 - d) * space + j) for d in range(2) for i, j in link]

    def over_dp(x):
        return lax.ppermute(x, "dp", swap)

    def over_pair(x):
        return lax.ppermute(x, "space", pair)

    def over_link(x):
        return lax.ppermute(x, "space", link)

    oth = over_dp(own)
    own2 = over_link(own)
    oth2 = lax.ppermute(own, ("dp", "space"), cross)
    we_there = over_dp(w_embed)
    own1 = over_pair(own)
    oth1 = over_pair(oth)

    wq_same = over_dp(lax.dynamic_slice(w_qkv, (core * half, half), (half, half)))
    wq_cross = over_pair(wq_same)
    w1_same = over_dp(lax.dynamic_slice(w_dec1, (core * half, 0), (half, half)))
    w1_cross = over_pair(w1_same)
    w2_there = over_dp(w_dec2)

    def block_of(index, size):
        side = index // size
        even = jnp.where(side == 0, 2, jnp.where(side == 1, 0, 1))
        odd = jnp.where(side == 0, 1, jnp.where(side == 1, 0, 2))
        return jnp.where(core == 0, even, odd), index % size

    block, slot = block_of(enc_index, slots)
    column = jnp.where(enc_index >= 0, block * slots + slot, -1).T.reshape(rows, 1)
    pick = (column == jnp.arange(3 * slots, dtype=jnp.int32)[None]).astype(BF16)
    present = jnp.broadcast_to((column >= 0).astype(F32), (rows, 128))

    block, slot = block_of(proc_index, nodes)
    near = jnp.arange(6 * nodes, dtype=jnp.int32)
    sample_of = (near // nodes) % 2
    code = (near // (2 * nodes)) * nodes + near % nodes
    column = (block * nodes + slot)[:, :, None] == code[None, None]
    times = jnp.sum(column.astype(F32), axis=1)
    times = jnp.concatenate(
        [times * (sample_of == 0)[None], times * (sample_of == 1)[None]], axis=0
    )

    block, slot = block_of(dec_index, nodes)
    column = (block * nodes + slot)[:, :, None] == jnp.arange(3 * nodes, dtype=jnp.int32)
    dec_count = jnp.sum(column.astype(F32), axis=1).astype(BF16)

    valid = (jnp.arange(slots, dtype=jnp.int32) < grid_count[0]).astype(F32)[:, None]
    area = area_weight[:, None]

    pairs, probs = call(
        encode_kernel,
        (
            jax.ShapeDtypeStruct((2 * rows, width), BF16),
            jax.ShapeDtypeStruct((HEADS, 2 * rows), BF16),
        ),
        (place, own, own1, own2, oth, oth1, oth2, pick, present, w_embed, we_there, w_enc_kv,
         mesh_query),
        flops=2 * 2 * rows * width * (width + field_count),
    )
    probs = over_dp(probs)
    latent = call(
        latent_kernel,
        jax.ShapeDtypeStruct((2 * nodes, width), BF16),
        (probs, pairs, mesh_query),
        flops=2 * 2 * rows * width * 128,
        smem=(),
    )
    came = over_dp(latent)
    came = jnp.concatenate([came[nodes:], came[:nodes]], axis=0)
    latent = jnp.where(row == 0, came, latent)
    lat1 = over_pair(latent)
    lat2 = over_link(latent)
    keep, send = call(
        mesh_kernel,
        (
            jax.ShapeDtypeStruct((nodes, width), F32),
            jax.ShapeDtypeStruct((nodes, width), BF16),
        ),
        (place, latent, lat1, lat2, times, w_qkv, wq_same, wq_cross, w_out),
        scratch=[pltpu.VMEM((6 * nodes, width), BF16)],
        flops=2 * 6 * nodes * width * 3 * half,
    )
    updated = (keep + over_dp(send).astype(F32)).astype(BF16)
    up1 = over_pair(updated)
    up2 = over_link(updated)
    predicted, sums = call(
        decode_kernel,
        (
            jax.ShapeDtypeStruct((slots, field_count), BF16),
            jax.ShapeDtypeStruct((space * samples, 8, field_count), F32),
        ),
        (place, updated, up1, up2, dec_count, w_dec1, w1_same, w1_cross, w_dec2, w2_there, own,
         target[0], area, valid),
        scratch=[pltpu.VMEM((slots, width), BF16)],
        flops=2 * slots * width * (width + field_count),
    )
    parts = lax.all_to_all(sums, ("dp", "space"), 0, 0)
    loss = call(
        loss_kernel, jax.ShapeDtypeStruct((1, 1), F32), (parts,), smem=()
    )
    return predicted[None], loss[0, 0]


def with_halo(cells, sides, width):
    for axis, dim in sides:
        count = lax.axis_size(axis)
        ends = count - 1
        head = lax.slice_in_dim(cells, 0, width, axis=dim)
        tail = lax.slice_in_dim(cells, cells.shape[dim] - width, cells.shape[dim], axis=dim)
        cells = jnp.concatenate(
            [
                lax.ppermute(tail, axis, [(i, (i + 1) % count) for i in range(ends)]),
                cells,
                lax.ppermute(head, axis, [((i + 1) % count, i) for i in range(ends)]),
            ],
            axis=dim,
        )
    return cells


def layer_norm(values):
    centre = jnp.mean(values, axis=-1, keepdims=True)
    shifted = values - centre
    spread = jnp.mean(shifted * shifted, axis=-1, keepdims=True)
    return shifted / jnp.sqrt(spread + 1e-05)


def attend(queries, gathered, present):
    node_count, width = queries.shape
    per_head_width = width // HEADS
    split_query_heads = queries.reshape(node_count, HEADS, per_head_width)
    split_key_heads = gathered[:, :, :width].reshape(node_count, -1, HEADS, per_head_width)
    split_value_heads = gathered[:, :, width:].reshape(node_count, -1, HEADS, per_head_width)
    attention_logits = jnp.einsum(
        "gtz,gxtz->gtx", split_query_heads, split_key_heads, preferred_element_type=jnp.float32
    ) / math.sqrt(per_head_width)
    attention_logits = jnp.where(present[:, None, :], attention_logits, -jnp.inf)
    attention_probs = jax.nn.softmax(attention_logits, axis=-1).astype(jnp.bfloat16)
    aggregated_values = jnp.einsum(
        "owi,oiwn->own", attention_probs, split_value_heads, preferred_element_type=jnp.float32
    )
    return aggregated_values.reshape(node_count, width)


def general_body(
    fields,
    target,
    area_weight,
    grid_count,
    mesh_query,
    enc_index,
    proc_index,
    dec_index,
    w_embed,
    w_enc_kv,
    w_qkv,
    w_out,
    w_dec1,
    w_dec2,
):
    own_fields = fields[0]
    grid_rows = own_fields.shape[0]
    mesh_rows, width = mesh_query.shape
    field_count = own_fields.shape[1]
    grid_window = with_halo(
        jax.nn.silu(
            jnp.dot(
                own_fields,
                lax.all_gather(w_embed, "dp", axis=1, tiled=True),
                preferred_element_type=jnp.float32,
            )
        ).astype(jnp.bfloat16),
        (("space", 0),),
        grid_rows,
    )
    grid_pairs = jnp.dot(
        grid_window,
        lax.all_gather(w_enc_kv, "dp", axis=1, tiled=True),
        preferred_element_type=jnp.float32,
    ).astype(jnp.bfloat16)
    present = enc_index >= 0
    enc_near = jnp.take(grid_pairs, jnp.maximum(enc_index, 0), axis=0)
    latent = (mesh_query.astype(jnp.float32) + attend(mesh_query, enc_near, present)).astype(
        jnp.bfloat16
    )
    normed = layer_norm(latent.astype(jnp.float32)).astype(jnp.bfloat16)
    mesh_qkv = jnp.dot(
        normed, lax.all_gather(w_qkv, "dp", axis=1, tiled=True), preferred_element_type=jnp.float32
    ).astype(jnp.bfloat16)
    mesh_queries = mesh_qkv[:, :width]
    mesh_pairs = with_halo(mesh_qkv[:, width:], (("space", 0),), mesh_rows)
    proc_near = jnp.take(mesh_pairs, proc_index, axis=0)
    mixed = attend(mesh_queries, proc_near, jnp.ones(proc_index.shape, dtype=bool)).astype(
        jnp.bfloat16
    )
    columns = mixed
    projected = jnp.dot(
        columns, lax.all_gather(w_out, "dp", axis=0, tiled=True), preferred_element_type=jnp.float32
    )
    updated = (latent.astype(jnp.float32) + projected).astype(jnp.bfloat16)
    mesh_window = with_halo(updated, (("space", 0),), mesh_rows)
    dec_near = jnp.take(mesh_window, dec_index, axis=0).astype(jnp.float32)
    decoder_in = layer_norm(jnp.mean(dec_near, axis=1)).astype(jnp.bfloat16)
    decoder_hidden = jax.nn.silu(
        jnp.dot(
            decoder_in,
            lax.all_gather(w_dec1, "dp", axis=1, tiled=True),
            preferred_element_type=jnp.float32,
        )
    ).astype(jnp.bfloat16)
    columns = decoder_hidden
    increment = jnp.dot(
        columns,
        lax.all_gather(w_dec2, "dp", axis=0, tiled=True),
        preferred_element_type=jnp.float32,
    )
    valid = jnp.arange(grid_rows, dtype=jnp.int32) < grid_count[0]
    predicted = jnp.where(
        valid[:, None], own_fields.astype(jnp.float32) + increment, jnp.float32(0.0)
    )
    keep_mask = valid.astype(jnp.float32)
    target_rows = target[0].astype(jnp.float32)
    misfit = predicted - target_rows
    error_sums = jnp.sum((keep_mask * area_weight)[:, None] * misfit * misfit, axis=0)
    target_sums = jnp.sum(keep_mask[:, None] * target_rows * target_rows, axis=0)
    valid_count = jnp.sum(keep_mask)
    weight_sum = jnp.sum(keep_mask * area_weight)
    target_all, count_all, weight_all = lax.psum(
        (target_sums, valid_count, weight_sum), ("dp", "space")
    )
    local_loss = jnp.sum(error_sums / (target_all / count_all + 1e-05))
    loss = lax.psum(local_loss, ("dp", "space")) / (field_count * weight_all)
    return (predicted.astype(jnp.bfloat16)[None], loss)


def solution(mesh):
    placed = (
        P("dp", "space", None),
        P("dp", "space", None),
        P("space"),
        P("space"),
        P("space", None),
        P("space", None),
        P("space", None),
        P("space", None),
        P(None, "dp"),
        P(None, "dp"),
        P(None, "dp"),
        P("dp", None),
        P(None, "dp"),
        P("dp", None),
    )
    small = mesh.shape["dp"] == 2 and mesh.shape["space"] % 2 == 0
    return jax.shard_map(
        small_body if small else general_body, mesh=mesh, in_specs=placed, out_specs=(P("dp", "space", None), P()), check_vma=False
    )
```

```python
import math

import jax
import jax.numpy as jnp
from jax import lax
from jax.experimental import pallas as pl
from jax.experimental.pallas import tpu as pltpu
from jax.sharding import PartitionSpec as P

HEADS = 16
F32 = jnp.float32
BF16 = jnp.bfloat16


def silu(x):
    return 0.5 * x * (1.0 + jnp.tanh(0.5 * x))


def dot(a, b):
    return jnp.dot(a, b, preferred_element_type=F32)


def dot_nt(a, b, precision=None):
    return lax.dot_general(
        a, b, (((1,), (1,)), ((), ())), preferred_element_type=F32, precision=precision
    )


def normalize(values):
    centre = jnp.mean(values, axis=-1, keepdims=True)
    shifted = values - centre
    spread = jnp.mean(shifted * shifted, axis=-1, keepdims=True)
    return shifted * lax.rsqrt(spread + 1e-05)


def shape(dims, dtype=BF16):
    return jax.ShapeDtypeStruct(tuple(dims), dtype)


def call(kernel, outs, args, scratch=(), flops=0, smem=()):
    size = sum(math.prod(a.shape) * a.dtype.itemsize for a in args)
    return pl.pallas_call(
        kernel,
        out_shape=tuple(outs),
        in_specs=[
            pl.BlockSpec(memory_space=pltpu.SMEM if i in smem else pltpu.VMEM)
            for i in range(len(args))
        ],
        out_specs=(pl.BlockSpec(memory_space=pltpu.VMEM),) * len(outs),
        scratch_shapes=list(scratch),
        compiler_params=pltpu.CompilerParams(vmem_limit_bytes=24 * 1024 * 1024),
        cost_estimate=pl.CostEstimate(flops=flops, bytes_accessed=size, transcendentals=0),
    )(*args)


def cut(w, column, width):
    pieces = 8
    size = w.shape[0] // 4
    step = size // pieces

    def kernel(w_ref, out_ref, sems):
        start = (lax.axis_index("space") % 4) * size
        copies = [
            pltpu.make_async_copy(
                w_ref.at[
                    pl.ds(pl.multiple_of(start + i * step, step), step), pl.ds(column, width)
                ],
                out_ref.at[pl.ds(i * step, step), :],
                sems.at[i],
            )
            for i in range(pieces)
        ]
        for copy in copies:
            copy.start()
        for copy in copies:
            copy.wait()

    return pl.pallas_call(
        kernel,
        out_shape=shape((size, width)),
        in_specs=[pl.BlockSpec(memory_space=pltpu.HBM)],
        out_specs=pl.BlockSpec(memory_space=pltpu.VMEM),
        scratch_shapes=[pltpu.SemaphoreType.DMA((pieces,))],
        compiler_params=pltpu.CompilerParams(vmem_limit_bytes=58 * 1024 * 1024),
        cost_estimate=pl.CostEstimate(flops=0, bytes_accessed=0, transcendentals=0),
    )(w)


def side_block(index, size):
    odd = lax.axis_index("space") % 2
    side = index // size
    block = jnp.where(side == 1, 0, jnp.where((side == 2) == (odd == 0), 1, 2))
    return block * size + index % size


def encode_kernel(
    query_ref, index_ref, own, own1, own2, oth, oth1, oth2, we_here, we_there, w_ref,
    pairs_ref, probs_ref,
):
    nodes, width = query_ref.shape
    entries = index_ref.shape[0]
    rows = nodes * entries
    per_head = width // HEADS
    ours = lax.axis_index("dp")
    index = jnp.transpose(index_ref[...])
    entry = jnp.concatenate([index[:, k : k + 1] for k in range(entries)], axis=0)
    head_of = lax.broadcasted_iota(jnp.int32, (width, 128), 0) // per_head
    fold = (head_of == lax.broadcasted_iota(jnp.int32, (width, 128), 1)).astype(BF16)
    queries = jnp.broadcast_to(query_ref[...].astype(F32)[None], (entries, nodes, width))
    queries = queries.reshape(rows, width)
    present = jnp.broadcast_to(entry >= 0, (rows, 128))
    slots = own.shape[1]
    place = jnp.where(entry >= 0, side_block(jnp.maximum(entry, 0), slots), -1)
    lane = lax.broadcasted_iota(jnp.int32, (rows, slots), 1)
    pick = [(place == lane + i * slots).astype(BF16) for i in range(3)]
    half = we_here.shape[1]
    here = pl.multiple_of(ours * half, half)
    there = pl.multiple_of((1 - ours) * half, half)
    for s in range(2):
        near = 0.0
        for i, (mine, theirs) in enumerate(((own, oth), (own1, oth1), (own2, oth2))):
            near += dot_nt(pick[i], jnp.where(ours == s, mine[...], theirs[...]))
        near = near.astype(BF16)
        embed_here = silu(dot(near, we_here[...])).astype(BF16)
        embed_there = silu(dot(near, we_there[...])).astype(BF16)
        pairs = dot(embed_here, w_ref[pl.ds(here, half), :])
        pairs = (pairs + dot(embed_there, w_ref[pl.ds(there, half), :])).astype(BF16)
        pairs_ref[s * rows : (s + 1) * rows, :] = pairs
        product = pairs.astype(F32) * queries
        high = product.astype(BF16)
        low = (product - high.astype(F32)).astype(BF16)
        logits = (dot(high, fold) + dot(low, fold)) * (1.0 / math.sqrt(per_head))
        logits = jnp.where(present, logits, -1e30).reshape(entries, nodes, 128)
        top = jnp.max(logits, axis=0, keepdims=True)
        weight = jnp.where(present.reshape(entries, nodes, 128), jnp.exp(logits - top), 0.0)
        weight = weight / jnp.sum(weight, axis=0, keepdims=True)
        turned = jnp.transpose(weight.reshape(rows, 128))
        probs_ref[:, s * rows : (s + 1) * rows] = turned[:HEADS].astype(BF16)


def latent_kernel(query_ref, probs, pairs, latent_ref):
    query = query_ref[...].astype(F32)
    nodes, width = query.shape
    rows = pairs.shape[0] // 2
    entries = rows // nodes
    per_head = width // HEADS
    head_of = lax.broadcasted_iota(jnp.int32, (HEADS, width), 1) // per_head
    spread = (head_of == lax.broadcasted_iota(jnp.int32, (HEADS, width), 0)).astype(BF16)
    for s in range(2):
        turned = probs[:, s * rows : (s + 1) * rows].astype(F32)
        weight = jnp.transpose(turned).astype(BF16)
        mixed = dot(weight, spread) * pairs[s * rows : (s + 1) * rows, :].astype(F32)
        mixed = jnp.sum(mixed.reshape(entries, nodes, width), axis=0)
        latent_ref[s * nodes : (s + 1) * nodes, :] = (query + mixed).astype(BF16)


def choose_kernel(mine, theirs, w_ref, out_ref, part_ref):
    first = lax.axis_index("dp") == 0
    out_ref[...] = jnp.where(first, theirs[...], mine[...])
    size = part_ref.shape[0]
    start = pl.multiple_of((lax.axis_index("space") % 4) * size, size)
    part_ref[...] = w_ref[pl.ds(start, size), :]


def add_kernel(mine, theirs, out_ref):
    out_ref[...] = (mine[...] + theirs[...].astype(F32)).astype(BF16)


def mesh_kernel(
    index_ref, lat0, lat1, lat2, w_ref, part0, part1, part2, part3, wo_ref,
    keep_ref, send_ref, norm_ref, sums_ref,
):
    both, width = lat0.shape
    nodes = both // 2
    half = width // 2
    rows = 3 * both
    heads = HEADS // 2
    per_head = half // heads
    place = side_block(jnp.transpose(index_ref[...]), nodes)
    near = lax.broadcasted_iota(jnp.int32, (nodes, rows), 1)
    code = (near // both) * nodes + near % nodes
    times = sum((place[:, j : j + 1] == code).astype(F32) for j in range(index_ref.shape[0]))
    second = (near // nodes) % 2
    times = jnp.concatenate(
        [jnp.where(second == 0, times, 0.0), jnp.where(second == 1, times, 0.0)], axis=0
    )[None]
    for i, block in enumerate((lat0, lat1, lat2)):
        norm_ref[i * both : (i + 1) * both, :] = normalize(block[...].astype(F32)).astype(BF16)
    spot = lax.axis_index("space") % 4
    ours = lax.axis_index("dp")
    first = ours == 0
    part_a = dot(norm_ref[...], w_ref[:, :half])
    part_c = dot(norm_ref[...], w_ref[:, 2 * half :])
    part_b = 0.0
    for i, block in enumerate((part0, part1, part2, part3)):
        size = block.shape[0]
        part = pl.multiple_of((spot ^ i) * size, size)
        part_b += dot(norm_ref[:, pl.ds(part, size)], block[...])
    queries = jnp.where(first, part_a[:both], part_b[:both]).astype(BF16)
    keys = jnp.where(first, part_c, part_a).astype(BF16)
    values = jnp.where(first, part_b, part_c).astype(BF16)
    head_of = lax.broadcasted_iota(jnp.int32, (both, half), 1) // per_head
    zero = jnp.zeros_like(queries)
    stacked = jnp.concatenate(
        [jnp.where(head_of == h, queries, zero) for h in range(heads)], axis=0
    )
    logits = dot_nt(stacked, keys) * (1.0 / math.sqrt(per_head))
    logits = logits.reshape(heads, both, rows)
    logits = jnp.where(times > 0, logits, -1e30)
    top = jnp.max(logits, axis=-1, keepdims=True)
    weight = times * jnp.exp(logits - top)
    weight = weight / jnp.sum(weight, axis=-1, keepdims=True)
    mixed = dot(weight.astype(BF16).reshape(heads * both, rows), values)
    mixed = mixed.reshape(heads, both, half)
    total = jnp.where(head_of == 0, mixed[0], 0.0)
    for h in range(1, heads):
        total = jnp.where(head_of == h, mixed[h], total)
    sums_ref[...] = dot(total.astype(BF16), wo_ref[...])
    mine = pl.multiple_of(ours * nodes, nodes)
    theirs = pl.multiple_of((1 - ours) * nodes, nodes)
    keep_ref[...] = lat0[pl.ds(mine, nodes), :].astype(F32) + sums_ref[pl.ds(mine, nodes), :]
    send_ref[...] = sums_ref[pl.ds(theirs, nodes), :].astype(BF16)


def decode_kernel(
    limit, index_ref, fields, target, area, up0, up1, up2,
    w1_ref, part0, part1, part2, part3, w2_ref, w2_there,
    pred_ref, sums_ref, norm_ref,
):
    count_field, slots = fields.shape
    keep = lax.broadcasted_iota(jnp.int32, (8, slots), 1) < limit[0]
    keep = keep.astype(F32)
    weight = keep * area[...]
    nodes, width = up0.shape
    entries = index_ref.shape[0]
    place = side_block(jnp.transpose(index_ref[...]), nodes)
    near = lax.broadcasted_iota(jnp.int32, (slots, nodes), 1)
    mean = 0.0
    for i, updated in enumerate((up0, up1, up2)):
        times = sum((place[:, k : k + 1] == near + i * nodes).astype(F32) for k in range(entries))
        mean += dot(times.astype(BF16), updated[...])
    norm_ref[...] = normalize(mean * (1.0 / entries)).astype(BF16)
    spot = lax.axis_index("space") % 4
    hidden = silu(dot(norm_ref[...], w1_ref[...])).astype(BF16)
    hidden_there = 0.0
    for i, block in enumerate((part0, part1, part2, part3)):
        size = block.shape[0]
        part = pl.multiple_of((spot ^ i) * size, size)
        hidden_there += dot(norm_ref[:, pl.ds(part, size)], block[...])
    hidden_there = silu(hidden_there).astype(BF16)
    increment = dot_nt(w2_ref[...], hidden) + dot_nt(w2_there[...], hidden_there)
    valid = keep[:1] > 0
    predicted = jnp.where(valid, fields[...].astype(F32) + increment, 0.0)
    pred_ref[...] = predicted.astype(BF16)
    goal = target[...].astype(F32)
    misfit = predicted - goal
    errors = dot_nt(weight, misfit * misfit, lax.Precision.HIGHEST)
    squares = dot_nt(keep, goal * goal, lax.Precision.HIGHEST)
    here_count = jnp.broadcast_to(jnp.sum(keep, axis=1, keepdims=True), (8, count_field))
    here_weight = jnp.broadcast_to(jnp.sum(weight, axis=1, keepdims=True), (8, count_field))
    row = lax.broadcasted_iota(jnp.int32, (8, count_field), 0)
    sums = jnp.where(
        row == 0, errors, jnp.where(row == 1, squares, jnp.where(row == 2, here_count, here_weight))
    )
    sums_ref[...] = jnp.broadcast_to(sums[None], sums_ref.shape)


def loss_kernel(parts, loss_ref):
    total = jnp.sum(parts[...], axis=0)
    fields = total.shape[1]
    scaled = total[0:1] / (total[1:2] / total[2:3] + 1e-05)
    weight = total[3:4, 0:1]
    loss_ref[...] = jnp.sum(scaled, axis=1, keepdims=True) / (fields * weight)


def small_body(
    fields, target, area_weight, grid_count, mesh_query, enc_index, proc_index, dec_index,
    w_embed, w_enc_kv, w_qkv, w_out, w_dec1, w_dec2,
):
    space = lax.axis_size("space")
    samples = lax.axis_size("dp")
    own = fields[0].T
    goal = target[0].T
    w2 = w_dec2.T
    field_count, slots = own.shape
    nodes, width = mesh_query.shape
    half = width // 2
    rows = nodes * enc_index.shape[1]

    swap = [(0, 1), (1, 0)]
    pair = [(i, i ^ 1) for i in range(space)]
    link = [(i, i + 1) for i in range(1, space - 1, 2)]
    link = link + [(j, i) for i, j in link]

    def over_dp(x):
        return lax.ppermute(x, "dp", swap)

    def over_pair(x):
        return lax.ppermute(x, "space", pair)

    def over_link(x):
        return lax.ppermute(x, "space", link)

    def over_both(x, steps):
        steps = [(d * space + i, (1 - d) * space + j) for d in range(2) for i, j in steps]
        return lax.ppermute(x, ("dp", "space"), steps)

    def over_quad(x):
        return lax.ppermute(x, "space", [(i, i ^ 2) for i in range(space)])

    def after(x, *others):
        return lax.optimization_barrier((x,) + others)[0]

    wq0 = cut(w_qkv, half, half)
    own = after(own, wq0)
    oth = over_dp(own)
    we_there = over_dp(w_embed)
    oth1 = over_both(own, pair)
    oth2 = over_both(own, link)
    own2 = over_link(own)
    own1 = over_pair(own)
    fetched = (own1, own2, oth2, oth1, we_there, oth, wq0)
    own1, own2, oth2, oth1, we_there, oth, wq0 = lax.optimization_barrier(fetched)
    wq0 = over_dp(wq0)

    pairs, probs = call(
        encode_kernel,
        (shape((2 * rows, width)), shape((HEADS, 2 * rows))),
        (mesh_query, enc_index.T, own, own1, own2, oth, oth1, oth2, w_embed, we_there, w_enc_kv),
        flops=2 * 2 * rows * width * (width + field_count),
    )
    (latent,) = call(
        latent_kernel,
        (shape((2 * nodes, width)),),
        (mesh_query, over_dp(probs), pairs),
        flops=2 * 2 * rows * width * 128,
    )
    came = over_dp(latent)
    wq0 = after(wq0, latent)
    wq2 = over_quad(wq0)
    wq1 = over_pair(after(wq0, came))
    wq3 = over_pair(after(wq2, came))
    latent, w10 = call(
        choose_kernel,
        (shape((2 * nodes, width)), shape((width // 4, half))),
        (latent, came, w_dec1),
    )
    lat1 = over_pair(latent)
    lat2 = over_link(latent)
    w10 = over_dp(w10)
    w2_there = over_dp(after(w2, latent))
    w10 = after(w10, lat2)
    w12 = over_quad(w10)
    keep, send = call(
        mesh_kernel,
        (shape((nodes, width), F32), shape((nodes, width))),
        (proc_index.T, latent, lat1, lat2, w_qkv, wq0, wq1, wq2, wq3, w_out),
        scratch=[pltpu.VMEM((6 * nodes, width), BF16), pltpu.VMEM((2 * nodes, width), F32)],
        flops=2 * 6 * nodes * width * 3 * half,
    )
    came = over_dp(send)
    w11 = over_pair(after(w10, keep))
    (updated,) = call(add_kernel, (shape((nodes, width)),), (keep, came))
    w13 = over_pair(after(w12, updated))
    predicted, sums = call(
        decode_kernel,
        (shape((field_count, slots)), shape((space * samples, 8, field_count), F32)),
        (grid_count, dec_index.T, own, goal, area_weight[None], updated, over_pair(updated),
         over_link(updated), w_dec1, w10, w11, w12, w13,
         w2, w2_there),
        scratch=[pltpu.VMEM((slots, width), BF16)],
        flops=2 * slots * width * (width + field_count),
        smem=(0,),
    )
    parts = lax.all_to_all(sums, ("dp", "space"), 0, 0)
    (loss,) = call(loss_kernel, (shape((1, 1), F32),), (parts,))
    return predicted.T[None], loss[0, 0]


def with_halo(cells, sides, width):
    for axis, dim in sides:
        count = lax.axis_size(axis)
        ends = count - 1
        head = lax.slice_in_dim(cells, 0, width, axis=dim)
        tail = lax.slice_in_dim(cells, cells.shape[dim] - width, cells.shape[dim], axis=dim)
        cells = jnp.concatenate(
            [
                lax.ppermute(tail, axis, [(i, (i + 1) % count) for i in range(ends)]),
                cells,
                lax.ppermute(head, axis, [((i + 1) % count, i) for i in range(ends)]),
            ],
            axis=dim,
        )
    return cells


def layer_norm(values):
    centre = jnp.mean(values, axis=-1, keepdims=True)
    shifted = values - centre
    spread = jnp.mean(shifted * shifted, axis=-1, keepdims=True)
    return shifted / jnp.sqrt(spread + 1e-05)


def attend(queries, gathered, present):
    node_count, width = queries.shape
    per_head_width = width // HEADS
    split_query_heads = queries.reshape(node_count, HEADS, per_head_width)
    split_key_heads = gathered[:, :, :width].reshape(node_count, -1, HEADS, per_head_width)
    split_value_heads = gathered[:, :, width:].reshape(node_count, -1, HEADS, per_head_width)
    attention_logits = jnp.einsum(
        "gtz,gxtz->gtx", split_query_heads, split_key_heads, preferred_element_type=jnp.float32
    ) / math.sqrt(per_head_width)
    attention_logits = jnp.where(present[:, None, :], attention_logits, -jnp.inf)
    attention_probs = jax.nn.softmax(attention_logits, axis=-1).astype(jnp.bfloat16)
    aggregated_values = jnp.einsum(
        "owi,oiwn->own", attention_probs, split_value_heads, preferred_element_type=jnp.float32
    )
    return aggregated_values.reshape(node_count, width)


def general_body(
    fields,
    target,
    area_weight,
    grid_count,
    mesh_query,
    enc_index,
    proc_index,
    dec_index,
    w_embed,
    w_enc_kv,
    w_qkv,
    w_out,
    w_dec1,
    w_dec2,
):
    own_fields = fields[0]
    grid_rows = own_fields.shape[0]
    mesh_rows, width = mesh_query.shape
    field_count = own_fields.shape[1]
    grid_window = with_halo(
        jax.nn.silu(
            jnp.dot(
                own_fields,
                lax.all_gather(w_embed, "dp", axis=1, tiled=True),
                preferred_element_type=jnp.float32,
            )
        ).astype(jnp.bfloat16),
        (("space", 0),),
        grid_rows,
    )
    grid_pairs = jnp.dot(
        grid_window,
        lax.all_gather(w_enc_kv, "dp", axis=1, tiled=True),
        preferred_element_type=jnp.float32,
    ).astype(jnp.bfloat16)
    present = enc_index >= 0
    enc_near = jnp.take(grid_pairs, jnp.maximum(enc_index, 0), axis=0)
    latent = (mesh_query.astype(jnp.float32) + attend(mesh_query, enc_near, present)).astype(
        jnp.bfloat16
    )
    normed = layer_norm(latent.astype(jnp.float32)).astype(jnp.bfloat16)
    mesh_qkv = jnp.dot(
        normed, lax.all_gather(w_qkv, "dp", axis=1, tiled=True), preferred_element_type=jnp.float32
    ).astype(jnp.bfloat16)
    mesh_queries = mesh_qkv[:, :width]
    mesh_pairs = with_halo(mesh_qkv[:, width:], (("space", 0),), mesh_rows)
    proc_near = jnp.take(mesh_pairs, proc_index, axis=0)
    mixed = attend(mesh_queries, proc_near, jnp.ones(proc_index.shape, dtype=bool)).astype(
        jnp.bfloat16
    )
    columns = mixed
    projected = jnp.dot(
        columns, lax.all_gather(w_out, "dp", axis=0, tiled=True), preferred_element_type=jnp.float32
    )
    updated = (latent.astype(jnp.float32) + projected).astype(jnp.bfloat16)
    mesh_window = with_halo(updated, (("space", 0),), mesh_rows)
    dec_near = jnp.take(mesh_window, dec_index, axis=0).astype(jnp.float32)
    decoder_in = layer_norm(jnp.mean(dec_near, axis=1)).astype(jnp.bfloat16)
    decoder_hidden = jax.nn.silu(
        jnp.dot(
            decoder_in,
            lax.all_gather(w_dec1, "dp", axis=1, tiled=True),
            preferred_element_type=jnp.float32,
        )
    ).astype(jnp.bfloat16)
    columns = decoder_hidden
    increment = jnp.dot(
        columns,
        lax.all_gather(w_dec2, "dp", axis=0, tiled=True),
        preferred_element_type=jnp.float32,
    )
    valid = jnp.arange(grid_rows, dtype=jnp.int32) < grid_count[0]
    predicted = jnp.where(
        valid[:, None], own_fields.astype(jnp.float32) + increment, jnp.float32(0.0)
    )
    keep_mask = valid.astype(jnp.float32)
    target_rows = target[0].astype(jnp.float32)
    misfit = predicted - target_rows
    error_sums = jnp.sum((keep_mask * area_weight)[:, None] * misfit * misfit, axis=0)
    target_sums = jnp.sum(keep_mask[:, None] * target_rows * target_rows, axis=0)
    valid_count = jnp.sum(keep_mask)
    weight_sum = jnp.sum(keep_mask * area_weight)
    target_all, count_all, weight_all = lax.psum(
        (target_sums, valid_count, weight_sum), ("dp", "space")
    )
    local_loss = jnp.sum(error_sums / (target_all / count_all + 1e-05))
    loss = lax.psum(local_loss, ("dp", "space")) / (field_count * weight_all)
    return (predicted.astype(jnp.bfloat16)[None], loss)


def solution(mesh):
    placed = (
        P("dp", "space", None),
        P("dp", "space", None),
        P("space"),
        P("space"),
        P("space", None),
        P("space", None),
        P("space", None),
        P("space", None),
        P(None, "dp"),
        P(None, "dp"),
        P(None, "dp"),
        P("dp", None),
        P(None, "dp"),
        P("dp", None),
    )
    small = mesh.shape["dp"] == 2 and mesh.shape["space"] % 4 == 0
    return jax.shard_map(
        small_body if small else general_body, mesh=mesh, in_specs=placed, out_specs=(P("dp", "space", None), P()), check_vma=False
    )
```

```python
import math

import jax
import jax.numpy as jnp
from jax import lax
from jax.experimental import pallas as pl
from jax.experimental.pallas import tpu as pltpu
from jax.sharding import PartitionSpec as P

HEADS = 16
F32 = jnp.float32
BF16 = jnp.bfloat16
BUSY = 4_000_000_000


def silu(x):
    return 0.5 * x * (1.0 + jnp.tanh(0.5 * x))


def dot(a, b):
    return jnp.dot(a, b, preferred_element_type=F32)


def dot_nt(a, b, precision=None):
    return lax.dot_general(
        a, b, (((1,), (1,)), ((), ())), preferred_element_type=F32, precision=precision
    )


def normalize(values):
    centre = jnp.mean(values, axis=-1, keepdims=True)
    shifted = values - centre
    spread = jnp.mean(shifted * shifted, axis=-1, keepdims=True)
    return shifted * lax.rsqrt(spread + 1e-05)


def shape(dims, dtype=BF16):
    return jax.ShapeDtypeStruct(tuple(dims), dtype)


def call(kernel, outs, args, scratch=(), flops=0, smem=()):
    size = sum(math.prod(a.shape) * a.dtype.itemsize for a in args)
    return pl.pallas_call(
        kernel,
        out_shape=tuple(outs),
        in_specs=[
            pl.BlockSpec(memory_space=pltpu.SMEM if i in smem else pltpu.VMEM)
            for i in range(len(args))
        ],
        out_specs=(pl.BlockSpec(memory_space=pltpu.VMEM),) * len(outs),
        scratch_shapes=list(scratch),
        compiler_params=pltpu.CompilerParams(vmem_limit_bytes=24 * 1024 * 1024),
        cost_estimate=pl.CostEstimate(flops=flops, bytes_accessed=size, transcendentals=0),
    )(*args)


def side_block(index, size):
    odd = lax.axis_index("space") % 2
    side = index // size
    block = jnp.where(side == 1, 0, jnp.where((side == 2) == (odd == 0), 1, 2))
    return block * size + index % size


def slots_of(index_ref, slots):
    entries = index_ref.shape[0]
    index = jnp.transpose(index_ref[...])
    entry = jnp.concatenate([index[:, k : k + 1] for k in range(entries)], axis=0)
    return jnp.where(entry >= 0, side_block(jnp.maximum(entry, 0), slots), -1), entry >= 0


def picked(place, i, slots):
    lane = lax.broadcasted_iota(jnp.int32, (place.shape[0], slots), 1)
    return (place == lane + i * slots).astype(BF16)


def pick_kernel(index_ref, pick_ref, present_ref):
    slots = pick_ref.shape[2]
    place, present = slots_of(index_ref, slots)
    for i in range(3):
        pick_ref[i] = picked(place, i, slots)
    present_ref[...] = jnp.broadcast_to(present.astype(F32), present_ref.shape)


def near_kernel(pick_ref, near0, near1, near2, out_ref):
    total = sum(dot_nt(block[...], pick_ref[i]) for i, block in enumerate((near0, near1, near2)))
    out_ref[...] = total.astype(BF16)


def encode(query_ref, present_ref, near_ref, we_here, we_there, w_ref, pairs_ref, probs_ref):
    nodes, width = query_ref.shape
    rows = present_ref.shape[0]
    entries = rows // nodes
    per_head = width // HEADS
    ours = lax.axis_index("dp")
    half = we_here.shape[1]
    here = pl.multiple_of(ours * half, half)
    there = pl.multiple_of((1 - ours) * half, half)
    near = jnp.transpose(near_ref[...].astype(F32)).astype(BF16)
    embed_here = silu(dot(near, we_here[...])).astype(BF16)
    embed_there = silu(dot(near, we_there[...])).astype(BF16)
    pairs = dot(embed_here, w_ref[pl.ds(here, half), :])
    pairs_ref[...] = (pairs + dot(embed_there, w_ref[pl.ds(there, half), :])).astype(BF16)

    @pl.when(ours == 0)
    def _():
        present = present_ref[...] > 0
        head_of = lax.broadcasted_iota(jnp.int32, (width, 128), 0) // per_head
        fold = (head_of == lax.broadcasted_iota(jnp.int32, (width, 128), 1)).astype(BF16)
        queries = jnp.broadcast_to(query_ref[...].astype(F32)[None], (entries, nodes, width))
        product = pairs_ref[...].astype(F32) * queries.reshape(rows, width)
        high = product.astype(BF16)
        low = (product - high.astype(F32)).astype(BF16)
        logits = (dot(high, fold) + dot(low, fold)) * (1.0 / math.sqrt(per_head))
        logits = jnp.where(present, logits, -1e30).reshape(entries, nodes, 128)
        top = jnp.max(logits, axis=0, keepdims=True)
        weight = jnp.where(present.reshape(entries, nodes, 128), jnp.exp(logits - top), 0.0)
        weight = weight / jnp.sum(weight, axis=0, keepdims=True)
        probs_ref[...] = jnp.transpose(weight.reshape(rows, 128))[:HEADS].astype(BF16)

    @pl.when(ours != 0)
    def _():
        probs_ref[...] = jnp.zeros(probs_ref.shape, BF16)


def encode_own_kernel(
    query_ref, present_ref, near_ref, we_here, we_there, w_ref, pairs_ref, probs_ref
):
    encode(query_ref, present_ref, near_ref, we_here, we_there, w_ref, pairs_ref, probs_ref)


def encode_other_kernel(
    query_ref, present_ref, near_ref, we_here, we_there, w_ref, first_ref, pairs_ref, probs_ref
):
    rows = first_ref.shape[1]
    probs_ref[:, :rows] = first_ref[...]
    encode(
        query_ref, present_ref, near_ref, we_here, we_there, w_ref, pairs_ref,
        probs_ref.at[:, rows : 2 * rows],
    )


def latent_kernel(query_ref, probs, pairs_own, pairs_other, latent_ref):
    query = query_ref[...].astype(F32)
    nodes, width = query.shape
    rows = pairs_own.shape[0]
    entries = rows // nodes
    per_head = width // HEADS
    head_of = lax.broadcasted_iota(jnp.int32, (HEADS, width), 1) // per_head
    spread = (head_of == lax.broadcasted_iota(jnp.int32, (HEADS, width), 0)).astype(BF16)

    @pl.when(lax.axis_index("dp") != 0)
    def _():
        for s, pairs in enumerate((pairs_other, pairs_own)):
            turned = probs[:, s * rows : (s + 1) * rows].astype(F32)
            weight = jnp.transpose(turned).astype(BF16)
            mixed = dot(weight, spread) * pairs[...].astype(F32)
            mixed = jnp.sum(mixed.reshape(entries, nodes, width), axis=0)
            latent_ref[s * nodes : (s + 1) * nodes, :] = (query + mixed).astype(BF16)

    @pl.when(lax.axis_index("dp") == 0)
    def _():
        latent_ref[...] = jnp.zeros_like(latent_ref)


def add_kernel(mine, theirs, out_ref):
    out_ref[...] = (mine[...] + theirs[...].astype(F32)).astype(BF16)


def later_kernel(latent, w_ref, send_ref, pairs_ref):
    half = w_ref.shape[1] // 3
    first = lax.axis_index("dp") == 0

    @pl.when(jnp.logical_not(first))
    def _():
        norm = normalize(latent[...].astype(F32)).astype(BF16)
        pairs_ref[:, :half] = dot(norm, w_ref[:, :half]).astype(BF16)
        send_ref[...] = dot(norm, w_ref[:, half : 2 * half]).astype(BF16)
        pairs_ref[:, half:] = dot(norm, w_ref[:, 2 * half :]).astype(BF16)

    @pl.when(first)
    def _():
        send_ref[...] = jnp.zeros(send_ref.shape, BF16)
        pairs_ref[...] = jnp.zeros(pairs_ref.shape, BF16)


def first_kernel(mine, came, w_ref, latent_ref, queries_ref, send_ref, keys_ref):
    half = w_ref.shape[1] // 3
    first = lax.axis_index("dp") == 0

    @pl.when(first)
    def _():
        latent_ref[...] = came[...]
        norm = normalize(came[...].astype(F32)).astype(BF16)
        queries_ref[...] = dot(norm, w_ref[:, :half]).astype(BF16)
        send_ref[...] = dot(norm, w_ref[:, half : 2 * half]).astype(BF16)
        keys_ref[...] = dot(norm, w_ref[:, 2 * half :]).astype(BF16)

    @pl.when(jnp.logical_not(first))
    def _():
        latent_ref[...] = mine[...]
        queries_ref[...] = jnp.zeros(queries_ref.shape, BF16)
        send_ref[...] = jnp.zeros(send_ref.shape, BF16)
        keys_ref[...] = jnp.zeros(keys_ref.shape, BF16)


def pairs_kernel(mine, keys, values, out_ref):
    half = keys.shape[1]
    first = lax.axis_index("dp") == 0
    out_ref[:, :half] = jnp.where(first, keys[...], mine[:, :half])
    out_ref[:, half:] = jnp.where(first, values[...], mine[:, half:])


def mesh_kernel(
    index_ref, latent, mine, came, pairs0, pairs1, pairs2, wo_ref, keep_ref, send_ref
):
    both, half = mine.shape
    nodes = both // 2
    rows = 3 * both
    heads = HEADS // 2
    per_head = half // heads
    first = lax.axis_index("dp") == 0
    queries = jnp.where(first, mine[...], came[...])
    pairs = jnp.concatenate([pairs0[...], pairs1[...], pairs2[...]], axis=0)
    keys, values = pairs[:, :half], pairs[:, half:]
    place = side_block(jnp.transpose(index_ref[...]), nodes)
    near = lax.broadcasted_iota(jnp.int32, (nodes, rows), 1)
    code = (near // both) * nodes + near % nodes
    times = sum((place[:, j : j + 1] == code).astype(F32) for j in range(index_ref.shape[0]))
    second = (near // nodes) % 2
    times = jnp.concatenate(
        [jnp.where(second == 0, times, 0.0), jnp.where(second == 1, times, 0.0)], axis=0
    )[None]
    head_of = lax.broadcasted_iota(jnp.int32, (both, half), 1) // per_head
    zero = jnp.zeros_like(queries)
    stacked = jnp.concatenate(
        [jnp.where(head_of == h, queries, zero) for h in range(heads)], axis=0
    )
    logits = dot_nt(stacked, keys) * (1.0 / math.sqrt(per_head))
    logits = logits.reshape(heads, both, rows)
    logits = jnp.where(times > 0, logits, -1e30)
    top = jnp.max(logits, axis=-1, keepdims=True)
    weight = times * jnp.exp(logits - top)
    weight = weight / jnp.sum(weight, axis=-1, keepdims=True)
    mixed = dot(weight.astype(BF16).reshape(heads * both, rows), values)
    mixed = mixed.reshape(heads, both, half)
    total = jnp.where(head_of == 0, mixed[0], 0.0)
    for h in range(1, heads):
        total = jnp.where(head_of == h, mixed[h], total)
    projected = dot(total.astype(BF16), wo_ref[...])
    keep_ref[...] = latent[...].astype(F32) + projected
    send_ref[...] = projected.astype(BF16)


def decode_kernel(index_ref, up0, up1, up2, w1_ref, w2_ref, keep_ref, send_ref):
    both, width = up0.shape
    nodes = both // 2
    entries, slots = index_ref.shape
    place = side_block(jnp.transpose(index_ref[...]), nodes)
    near = lax.broadcasted_iota(jnp.int32, (slots, nodes), 1)
    means = [0.0, 0.0]
    for i, block in enumerate((up0, up1, up2)):
        times = sum((place[:, k : k + 1] == near + i * nodes).astype(F32) for k in range(entries))
        for s in range(2):
            means[s] += dot(times.astype(BF16), block[s * nodes : (s + 1) * nodes, :])
    mean = jnp.concatenate(means, axis=0) * (1.0 / entries)
    hidden = silu(dot(normalize(mean).astype(BF16), w1_ref[...])).astype(BF16)
    parts = [dot_nt(w2_ref[...], hidden[s * slots : (s + 1) * slots]) for s in range(2)]
    first = lax.axis_index("dp") == 0
    keep_ref[...] = jnp.where(first, parts[0], parts[1])
    send_ref[...] = jnp.where(first, parts[1], parts[0]).astype(BF16)


def errors_kernel(limit, fields, target, area, keep_ref, came, pred_ref, sums_ref):
    count_field, slots = fields.shape
    keep = lax.broadcasted_iota(jnp.int32, (8, slots), 1) < limit[0]
    keep = keep.astype(F32)
    weight = keep * area[...]
    increment = keep_ref[...] + came[...].astype(F32)
    valid = keep[:1] > 0
    predicted = jnp.where(valid, fields[...].astype(F32) + increment, 0.0)
    pred_ref[...] = predicted.astype(BF16)
    goal = target[...].astype(F32)
    misfit = predicted - goal
    errors = dot_nt(weight, misfit * misfit, lax.Precision.HIGHEST)
    squares = dot_nt(keep, goal * goal, lax.Precision.HIGHEST)
    here_count = jnp.broadcast_to(jnp.sum(keep, axis=1, keepdims=True), (8, count_field))
    here_weight = jnp.broadcast_to(jnp.sum(weight, axis=1, keepdims=True), (8, count_field))
    row = lax.broadcasted_iota(jnp.int32, (8, count_field), 0)
    sums = jnp.where(
        row == 0, errors, jnp.where(row == 1, squares, jnp.where(row == 2, here_count, here_weight))
    )
    sums_ref[...] = jnp.broadcast_to(sums[None], sums_ref.shape)


def loss_kernel(parts, loss_ref):
    total = jnp.sum(parts[...], axis=0)
    fields = total.shape[1]
    scaled = total[0:1] / (total[1:2] / total[2:3] + 1e-05)
    weight = total[3:4, 0:1]
    loss_ref[...] = jnp.sum(scaled, axis=1, keepdims=True) / (fields * weight)


def small_body(
    fields, target, area_weight, grid_count, mesh_query, enc_index, proc_index, dec_index,
    w_embed, w_enc_kv, w_qkv, w_out, w_dec1, w_dec2,
):
    space = lax.axis_size("space")
    samples = lax.axis_size("dp")
    own = fields[0].T
    goal = target[0].T
    w2 = w_dec2.T
    field_count, slots = own.shape
    nodes, width = mesh_query.shape
    half = width // 2
    rows = nodes * enc_index.shape[1]

    swap = [(0, 1), (1, 0)]
    pair = [(i, i ^ 1) for i in range(space)]
    link = [(i, i + 1) for i in range(1, space - 1, 2)]
    link = link + [(j, i) for i, j in link]

    def over_dp(x):
        return lax.ppermute(x, "dp", swap)

    def to_first(x):
        return lax.ppermute(x, "dp", [(1, 0)])

    def to_second(x):
        return lax.ppermute(x, "dp", [(0, 1)])

    def over_pair(x):
        return lax.ppermute(x, "space", pair)

    def over_link(x):
        return lax.ppermute(x, "space", link)

    def over_both(x, steps):
        steps = [(d * space + i, (1 - d) * space + j) for d in range(2) for i, j in steps]
        return lax.ppermute(x, ("dp", "space"), steps)

    def over_quad(x):
        return lax.ppermute(x, "space", [(i, i ^ 2) for i in range(space)])

    def after(x, *others):
        return lax.optimization_barrier((x,) + others)[0]

    we_there = over_dp(w_embed)
    own1 = over_pair(own)
    own2 = over_link(own)
    pick, present = call(
        pick_kernel,
        (shape((3, rows, slots)), shape((rows, 128), F32)),
        (enc_index.T,),
        flops=BUSY,
    )
    (near,) = call(
        near_kernel, (shape((field_count, rows)),), (pick, own, own1, own2), flops=BUSY
    )
    other = over_dp(near)
    pairs_own, probs = call(
        encode_own_kernel,
        (shape((rows, width)), shape((HEADS, rows))),
        (mesh_query, present, near, w_embed, we_there, w_enc_kv),
        flops=2 * rows * width * (width + field_count),
    )
    pairs, probs = call(
        encode_other_kernel,
        (shape((rows, width)), shape((HEADS, 2 * rows))),
        (mesh_query, present, other, w_embed, we_there, w_enc_kv, probs),
        flops=2 * rows * width * (width + field_count),
    )
    (latent,) = call(
        latent_kernel,
        (shape((2 * nodes, width)),),
        (mesh_query, to_second(probs), pairs_own, pairs),
        flops=2 * 2 * rows * width * 128,
    )
    came = to_first(latent)
    send, pairs = call(
        later_kernel,
        (shape((2 * nodes, half)), shape((2 * nodes, width))),
        (latent, w_qkv),
        flops=2 * 2 * nodes * width * 3 * half,
    )
    values = to_first(send)
    latent, queries, send, keys = call(
        first_kernel,
        (shape((2 * nodes, width)),) + (shape((2 * nodes, half)),) * 3,
        (latent, came, w_qkv),
        flops=2 * 2 * nodes * width * 3 * half,
    )
    (pairs,) = call(pairs_kernel, (shape((2 * nodes, width)),), (pairs, keys, values))
    keep, send = call(
        mesh_kernel,
        (shape((2 * nodes, width), F32), shape((2 * nodes, width))),
        (proc_index.T, latent, queries, to_second(send), pairs, over_pair(pairs),
         over_link(pairs), w_out),
        flops=2 * 2 * nodes * width * width,
    )
    (updated,) = call(add_kernel, (shape((2 * nodes, width)),), (keep, over_dp(send)))
    up2 = over_link(updated)
    keep, send = call(
        decode_kernel,
        (shape((field_count, slots), F32), shape((field_count, slots))),
        (dec_index.T, updated, over_pair(updated), up2, w_dec1, w2),
        flops=2 * slots * width * (width + field_count),
    )
    predicted, sums = call(
        errors_kernel,
        (shape((field_count, slots)), shape((space * samples, 8, field_count), F32)),
        (grid_count, own, goal, area_weight[None], keep, over_dp(send)),
        smem=(0,),
    )
    parts = lax.all_to_all(sums, ("dp", "space"), 0, 0)
    (loss,) = call(loss_kernel, (shape((1, 1), F32),), (parts,))
    return predicted.T[None], loss[0, 0]


def with_halo(cells, sides, width):
    for axis, dim in sides:
        count = lax.axis_size(axis)
        ends = count - 1
        head = lax.slice_in_dim(cells, 0, width, axis=dim)
        tail = lax.slice_in_dim(cells, cells.shape[dim] - width, cells.shape[dim], axis=dim)
        cells = jnp.concatenate(
            [
                lax.ppermute(tail, axis, [(i, (i + 1) % count) for i in range(ends)]),
                cells,
                lax.ppermute(head, axis, [((i + 1) % count, i) for i in range(ends)]),
            ],
            axis=dim,
        )
    return cells


def layer_norm(values):
    centre = jnp.mean(values, axis=-1, keepdims=True)
    shifted = values - centre
    spread = jnp.mean(shifted * shifted, axis=-1, keepdims=True)
    return shifted / jnp.sqrt(spread + 1e-05)


def attend(queries, gathered, present):
    node_count, width = queries.shape
    per_head_width = width // HEADS
    split_query_heads = queries.reshape(node_count, HEADS, per_head_width)
    split_key_heads = gathered[:, :, :width].reshape(node_count, -1, HEADS, per_head_width)
    split_value_heads = gathered[:, :, width:].reshape(node_count, -1, HEADS, per_head_width)
    attention_logits = jnp.einsum(
        "gtz,gxtz->gtx", split_query_heads, split_key_heads, preferred_element_type=jnp.float32
    ) / math.sqrt(per_head_width)
    attention_logits = jnp.where(present[:, None, :], attention_logits, -jnp.inf)
    attention_probs = jax.nn.softmax(attention_logits, axis=-1).astype(jnp.bfloat16)
    aggregated_values = jnp.einsum(
        "owi,oiwn->own", attention_probs, split_value_heads, preferred_element_type=jnp.float32
    )
    return aggregated_values.reshape(node_count, width)


def general_body(
    fields,
    target,
    area_weight,
    grid_count,
    mesh_query,
    enc_index,
    proc_index,
    dec_index,
    w_embed,
    w_enc_kv,
    w_qkv,
    w_out,
    w_dec1,
    w_dec2,
):
    own_fields = fields[0]
    grid_rows = own_fields.shape[0]
    mesh_rows, width = mesh_query.shape
    field_count = own_fields.shape[1]
    grid_window = with_halo(
        jax.nn.silu(
            jnp.dot(
                own_fields,
                lax.all_gather(w_embed, "dp", axis=1, tiled=True),
                preferred_element_type=jnp.float32,
            )
        ).astype(jnp.bfloat16),
        (("space", 0),),
        grid_rows,
    )
    grid_pairs = jnp.dot(
        grid_window,
        lax.all_gather(w_enc_kv, "dp", axis=1, tiled=True),
        preferred_element_type=jnp.float32,
    ).astype(jnp.bfloat16)
    present = enc_index >= 0
    enc_near = jnp.take(grid_pairs, jnp.maximum(enc_index, 0), axis=0)
    latent = (mesh_query.astype(jnp.float32) + attend(mesh_query, enc_near, present)).astype(
        jnp.bfloat16
    )
    normed = layer_norm(latent.astype(jnp.float32)).astype(jnp.bfloat16)
    mesh_qkv = jnp.dot(
        normed, lax.all_gather(w_qkv, "dp", axis=1, tiled=True), preferred_element_type=jnp.float32
    ).astype(jnp.bfloat16)
    mesh_queries = mesh_qkv[:, :width]
    mesh_pairs = with_halo(mesh_qkv[:, width:], (("space", 0),), mesh_rows)
    proc_near = jnp.take(mesh_pairs, proc_index, axis=0)
    mixed = attend(mesh_queries, proc_near, jnp.ones(proc_index.shape, dtype=bool)).astype(
        jnp.bfloat16
    )
    columns = mixed
    projected = jnp.dot(
        columns, lax.all_gather(w_out, "dp", axis=0, tiled=True), preferred_element_type=jnp.float32
    )
    updated = (latent.astype(jnp.float32) + projected).astype(jnp.bfloat16)
    mesh_window = with_halo(updated, (("space", 0),), mesh_rows)
    dec_near = jnp.take(mesh_window, dec_index, axis=0).astype(jnp.float32)
    decoder_in = layer_norm(jnp.mean(dec_near, axis=1)).astype(jnp.bfloat16)
    decoder_hidden = jax.nn.silu(
        jnp.dot(
            decoder_in,
            lax.all_gather(w_dec1, "dp", axis=1, tiled=True),
            preferred_element_type=jnp.float32,
        )
    ).astype(jnp.bfloat16)
    columns = decoder_hidden
    increment = jnp.dot(
        columns,
        lax.all_gather(w_dec2, "dp", axis=0, tiled=True),
        preferred_element_type=jnp.float32,
    )
    valid = jnp.arange(grid_rows, dtype=jnp.int32) < grid_count[0]
    predicted = jnp.where(
        valid[:, None], own_fields.astype(jnp.float32) + increment, jnp.float32(0.0)
    )
    keep_mask = valid.astype(jnp.float32)
    target_rows = target[0].astype(jnp.float32)
    misfit = predicted - target_rows
    error_sums = jnp.sum((keep_mask * area_weight)[:, None] * misfit * misfit, axis=0)
    target_sums = jnp.sum(keep_mask[:, None] * target_rows * target_rows, axis=0)
    valid_count = jnp.sum(keep_mask)
    weight_sum = jnp.sum(keep_mask * area_weight)
    target_all, count_all, weight_all = lax.psum(
        (target_sums, valid_count, weight_sum), ("dp", "space")
    )
    local_loss = jnp.sum(error_sums / (target_all / count_all + 1e-05))
    loss = lax.psum(local_loss, ("dp", "space")) / (field_count * weight_all)
    return (predicted.astype(jnp.bfloat16)[None], loss)


def solution(mesh):
    placed = (
        P("dp", "space", None),
        P("dp", "space", None),
        P("space"),
        P("space"),
        P("space", None),
        P("space", None),
        P("space", None),
        P("space", None),
        P(None, "dp"),
        P(None, "dp"),
        P(None, "dp"),
        P("dp", None),
        P(None, "dp"),
        P("dp", None),
    )
    small = mesh.shape["dp"] == 2 and mesh.shape["space"] % 2 == 0
    return jax.shard_map(
        small_body if small else general_body, mesh=mesh, in_specs=placed, out_specs=(P("dp", "space", None), P()), check_vma=False
    )
```

```python
import functools
import math

import jax
import jax.numpy as jnp
from jax import lax
from jax.experimental import pallas as pl
from jax.experimental.pallas import tpu as pltpu
from jax.sharding import PartitionSpec as P

HEADS = 16
F32 = jnp.float32
BF16 = jnp.bfloat16
BUSY = 4_000_000_000


def silu(x):
    return 0.5 * x * (1.0 + jnp.tanh(0.5 * x))


def dot(a, b):
    return jnp.dot(a, b, preferred_element_type=F32)


def dot_nt(a, b, precision=None):
    return lax.dot_general(
        a, b, (((1,), (1,)), ((), ())), preferred_element_type=F32, precision=precision
    )


def normalize(values):
    centre = jnp.mean(values, axis=-1, keepdims=True)
    shifted = values - centre
    spread = jnp.mean(shifted * shifted, axis=-1, keepdims=True)
    return shifted * lax.rsqrt(spread + 1e-05)


def shape(dims, dtype=BF16):
    return jax.ShapeDtypeStruct(tuple(dims), dtype)


def call(kernel, outs, args, scratch=(), flops=0, smem=(), size=None):
    size = size if size is not None else sum(math.prod(a.shape) * a.dtype.itemsize for a in args)
    return pl.pallas_call(
        kernel,
        out_shape=tuple(outs),
        in_specs=[
            pl.BlockSpec(memory_space=pltpu.SMEM if i in smem else pltpu.VMEM)
            for i in range(len(args))
        ],
        out_specs=(pl.BlockSpec(memory_space=pltpu.VMEM),) * len(outs),
        scratch_shapes=list(scratch),
        compiler_params=pltpu.CompilerParams(vmem_limit_bytes=24 * 1024 * 1024),
        cost_estimate=pl.CostEstimate(flops=flops, bytes_accessed=size, transcendentals=0),
    )(*args)


def side_block(index, size):
    odd = lax.axis_index("space") % 2
    side = index // size
    block = jnp.where(side == 1, 0, jnp.where((side == 2) == (odd == 0), 1, 2))
    return block * size + index % size


def slots_of(index_ref, slots):
    entries = index_ref.shape[0]
    index = jnp.transpose(index_ref[...])
    entry = jnp.concatenate([index[:, k : k + 1] for k in range(entries)], axis=0)
    return jnp.where(entry >= 0, side_block(jnp.maximum(entry, 0), slots), -1), entry >= 0


def picked(place, i, slots):
    lane = lax.broadcasted_iota(jnp.int32, (place.shape[0], slots), 1)
    return (place == lane + i * slots).astype(BF16)


def pick_kernel(index_ref, pick_ref, present_ref):
    slots = pick_ref.shape[2]
    place, present = slots_of(index_ref, slots)
    for i in range(3):
        pick_ref[i] = picked(place, i, slots)
    present_ref[...] = jnp.broadcast_to(present.astype(F32), present_ref.shape)


def share_kernel(w1_ref, w2_ref, out_ref, pad_ref):
    size = w1_ref.shape[0] // 8
    tail = pad_ref.shape[0] // 8
    spot = lax.axis_index("space")
    share = (spot % 2) * 4 + ((spot // 2) % 2) * 2 + (spot // 4) % 2
    pad_ref[...] = jnp.zeros(pad_ref.shape, BF16)
    pad_ref[: w2_ref.shape[0], :] = w2_ref[...]
    out_ref[:size, :] = w1_ref[pl.ds(pl.multiple_of(share * size, size), size), :]
    out_ref[size:, :] = pad_ref[pl.ds(pl.multiple_of(share * tail, tail), tail), :]


def join_kernel(step, tail, mine, theirs, out_ref):
    rows = mine.shape[0]
    bit = (lax.axis_index("space") // step) % 2
    for block, place in ((mine, bit), (theirs, 1 - bit)):
        size = rows - tail
        out_ref[pl.ds(pl.multiple_of(place * size, 16), size), :] = block[:size, :]
        start = pl.multiple_of(2 * size + place * tail, 16)
        out_ref[pl.ds(start, tail), :] = block[size:, :]


def near_kernel(pick_ref, near0, near1, near2, out_ref):
    total = sum(dot_nt(block[...], pick_ref[i]) for i, block in enumerate((near0, near1, near2)))
    out_ref[...] = total.astype(BF16)


def encode(query_ref, present_ref, near_ref, we_here, we_there, w_ref, pairs_ref, probs_ref):
    nodes, width = query_ref.shape
    rows = present_ref.shape[0]
    entries = rows // nodes
    per_head = width // HEADS
    ours = lax.axis_index("dp")
    half = we_here.shape[1]
    here = pl.multiple_of(ours * half, half)
    there = pl.multiple_of((1 - ours) * half, half)
    near = jnp.transpose(near_ref[...].astype(F32)).astype(BF16)
    embed_here = silu(dot(near, we_here[...])).astype(BF16)
    embed_there = silu(dot(near, we_there[...])).astype(BF16)
    pairs = dot(embed_here, w_ref[pl.ds(here, half), :])
    pairs_ref[...] = (pairs + dot(embed_there, w_ref[pl.ds(there, half), :])).astype(BF16)

    @pl.when(ours == 0)
    def _():
        present = present_ref[...] > 0
        head_of = lax.broadcasted_iota(jnp.int32, (width, 128), 0) // per_head
        fold = (head_of == lax.broadcasted_iota(jnp.int32, (width, 128), 1)).astype(BF16)
        queries = jnp.broadcast_to(query_ref[...].astype(F32)[None], (entries, nodes, width))
        product = pairs_ref[...].astype(F32) * queries.reshape(rows, width)
        high = product.astype(BF16)
        low = (product - high.astype(F32)).astype(BF16)
        logits = (dot(high, fold) + dot(low, fold)) * (1.0 / math.sqrt(per_head))
        logits = jnp.where(present, logits, -1e30).reshape(entries, nodes, 128)
        top = jnp.max(logits, axis=0, keepdims=True)
        weight = jnp.where(present.reshape(entries, nodes, 128), jnp.exp(logits - top), 0.0)
        weight = weight / jnp.sum(weight, axis=0, keepdims=True)
        probs_ref[...] = jnp.transpose(weight.reshape(rows, 128))[:HEADS].astype(BF16)

    @pl.when(ours != 0)
    def _():
        probs_ref[...] = jnp.zeros(probs_ref.shape, BF16)


def encode_own_kernel(
    query_ref, present_ref, near_ref, we_here, we_there, w_ref, pairs_ref, probs_ref
):
    encode(query_ref, present_ref, near_ref, we_here, we_there, w_ref, pairs_ref, probs_ref)


def encode_other_kernel(
    query_ref, present_ref, near_ref, we_here, we_there, w_ref, first_ref, pairs_ref, probs_ref
):
    rows = first_ref.shape[1]
    probs_ref[:, :rows] = first_ref[...]
    encode(
        query_ref, present_ref, near_ref, we_here, we_there, w_ref, pairs_ref,
        probs_ref.at[:, rows : 2 * rows],
    )


def latent_kernel(query_ref, probs, pairs_own, pairs_other, latent_ref):
    query = query_ref[...].astype(F32)
    nodes, width = query.shape
    rows = pairs_own.shape[0]
    entries = rows // nodes
    per_head = width // HEADS
    head_of = lax.broadcasted_iota(jnp.int32, (HEADS, width), 1) // per_head
    spread = (head_of == lax.broadcasted_iota(jnp.int32, (HEADS, width), 0)).astype(BF16)

    @pl.when(lax.axis_index("dp") != 0)
    def _():
        for s, pairs in enumerate((pairs_other, pairs_own)):
            turned = probs[:, s * rows : (s + 1) * rows].astype(F32)
            weight = jnp.transpose(turned).astype(BF16)
            mixed = dot(weight, spread) * pairs[...].astype(F32)
            mixed = jnp.sum(mixed.reshape(entries, nodes, width), axis=0)
            latent_ref[s * nodes : (s + 1) * nodes, :] = (query + mixed).astype(BF16)

    @pl.when(lax.axis_index("dp") == 0)
    def _():
        latent_ref[...] = jnp.zeros_like(latent_ref)


def add_kernel(mine, theirs, out_ref):
    out_ref[...] = (mine[...] + theirs[...].astype(F32)).astype(BF16)


def later_kernel(latent, w_ref, send_ref, pairs_ref):
    half = w_ref.shape[1] // 3
    first = lax.axis_index("dp") == 0

    @pl.when(jnp.logical_not(first))
    def _():
        norm = normalize(latent[...].astype(F32)).astype(BF16)
        pairs_ref[:, :half] = dot(norm, w_ref[:, :half]).astype(BF16)
        send_ref[...] = dot(norm, w_ref[:, half : 2 * half]).astype(BF16)
        pairs_ref[:, half:] = dot(norm, w_ref[:, 2 * half :]).astype(BF16)

    @pl.when(first)
    def _():
        send_ref[...] = jnp.zeros(send_ref.shape, BF16)
        pairs_ref[...] = jnp.zeros(pairs_ref.shape, BF16)


def first_kernel(mine, came, w_ref, latent_ref, queries_ref, send_ref, keys_ref):
    half = w_ref.shape[1] // 3
    first = lax.axis_index("dp") == 0

    @pl.when(first)
    def _():
        latent_ref[...] = came[...]
        norm = normalize(came[...].astype(F32)).astype(BF16)
        queries_ref[...] = dot(norm, w_ref[:, :half]).astype(BF16)
        send_ref[...] = dot(norm, w_ref[:, half : 2 * half]).astype(BF16)
        keys_ref[...] = dot(norm, w_ref[:, 2 * half :]).astype(BF16)

    @pl.when(jnp.logical_not(first))
    def _():
        latent_ref[...] = mine[...]
        queries_ref[...] = jnp.zeros(queries_ref.shape, BF16)
        send_ref[...] = jnp.zeros(send_ref.shape, BF16)
        keys_ref[...] = jnp.zeros(keys_ref.shape, BF16)


def pairs_kernel(mine, keys, values, out_ref):
    half = keys.shape[1]
    first = lax.axis_index("dp") == 0
    out_ref[:, :half] = jnp.where(first, keys[...], mine[:, :half])
    out_ref[:, half:] = jnp.where(first, values[...], mine[:, half:])


def mesh_kernel(
    index_ref, latent, mine, came, pairs0, pairs1, pairs2, wo_ref, keep_ref, send_ref, sums_ref
):
    both, half = mine.shape
    nodes = both // 2
    rows = 3 * both
    heads = HEADS // 2
    per_head = half // heads
    first = lax.axis_index("dp") == 0
    queries = jnp.where(first, mine[...], came[...])
    pairs = jnp.concatenate([pairs0[...], pairs1[...], pairs2[...]], axis=0)
    keys, values = pairs[:, :half], pairs[:, half:]
    place = side_block(jnp.transpose(index_ref[...]), nodes)
    near = lax.broadcasted_iota(jnp.int32, (nodes, rows), 1)
    code = (near // both) * nodes + near % nodes
    times = sum((place[:, j : j + 1] == code).astype(F32) for j in range(index_ref.shape[0]))
    second = (near // nodes) % 2
    times = jnp.concatenate(
        [jnp.where(second == 0, times, 0.0), jnp.where(second == 1, times, 0.0)], axis=0
    )[None]
    head_of = lax.broadcasted_iota(jnp.int32, (both, half), 1) // per_head
    zero = jnp.zeros_like(queries)
    stacked = jnp.concatenate(
        [jnp.where(head_of == h, queries, zero) for h in range(heads)], axis=0
    )
    logits = dot_nt(stacked, keys) * (1.0 / math.sqrt(per_head))
    logits = logits.reshape(heads, both, rows)
    logits = jnp.where(times > 0, logits, -1e30)
    top = jnp.max(logits, axis=-1, keepdims=True)
    weight = times * jnp.exp(logits - top)
    weight = weight / jnp.sum(weight, axis=-1, keepdims=True)
    mixed = dot(weight.astype(BF16).reshape(heads * both, rows), values)
    mixed = mixed.reshape(heads, both, half)
    total = jnp.where(head_of == 0, mixed[0], 0.0)
    for h in range(1, heads):
        total = jnp.where(head_of == h, mixed[h], total)
    sums_ref[...] = dot(total.astype(BF16), wo_ref[...])
    ours = lax.axis_index("dp")
    mine = pl.multiple_of(ours * nodes, nodes)
    theirs = pl.multiple_of((1 - ours) * nodes, nodes)
    keep_ref[...] = latent[pl.ds(mine, nodes), :].astype(F32) + sums_ref[pl.ds(mine, nodes), :]
    send_ref[...] = sums_ref[pl.ds(theirs, nodes), :].astype(BF16)


def decode_kernel(
    limit, index_ref, fields, target, area, up0, up1, up2,
    w1_ref, part0, part1, w2_ref,
    pred_ref, sums_ref, norm_ref, there_ref,
):
    count_field, slots = fields.shape
    keep = lax.broadcasted_iota(jnp.int32, (8, slots), 1) < limit[0]
    keep = keep.astype(F32)
    weight = keep * area[...]
    nodes, width = up0.shape
    entries = index_ref.shape[0]
    place = side_block(jnp.transpose(index_ref[...]), nodes)
    near = lax.broadcasted_iota(jnp.int32, (slots, nodes), 1)
    mean = 0.0
    for i, updated in enumerate((up0, up1, up2)):
        times = sum((place[:, k : k + 1] == near + i * nodes).astype(F32) for k in range(entries))
        mean += dot(times.astype(BF16), updated[...])
    norm_ref[...] = normalize(mean * (1.0 / entries)).astype(BF16)
    core = lax.axis_index("space") % 2
    hidden = silu(dot(norm_ref[...], w1_ref[...])).astype(BF16)
    hidden_there = 0.0
    size = width // 2
    tail = part0.shape[0] - size
    for i, block in enumerate((part0, part1)):
        part = pl.multiple_of((core ^ i) * size, size)
        hidden_there += dot(norm_ref[:, pl.ds(part, size)], block[:size, :])
        start = pl.multiple_of((core ^ i) * tail, tail)
        there_ref[pl.ds(start, tail), :] = block[size:, :]
    hidden_there = silu(hidden_there).astype(BF16)
    increment = dot_nt(w2_ref[...], hidden)
    increment += dot_nt(there_ref[:count_field, :], hidden_there)
    valid = keep[:1] > 0
    predicted = jnp.where(valid, fields[...].astype(F32) + increment, 0.0)
    pred_ref[...] = predicted.astype(BF16)
    goal = target[...].astype(F32)
    misfit = predicted - goal
    errors = dot_nt(weight, misfit * misfit, lax.Precision.HIGHEST)
    squares = dot_nt(keep, goal * goal, lax.Precision.HIGHEST)
    here_count = jnp.broadcast_to(jnp.sum(keep, axis=1, keepdims=True), (8, count_field))
    here_weight = jnp.broadcast_to(jnp.sum(weight, axis=1, keepdims=True), (8, count_field))
    row = lax.broadcasted_iota(jnp.int32, (8, count_field), 0)
    sums = jnp.where(
        row == 0, errors, jnp.where(row == 1, squares, jnp.where(row == 2, here_count, here_weight))
    )
    sums_ref[...] = jnp.broadcast_to(sums[None], sums_ref.shape)


def loss_kernel(parts, loss_ref):
    total = jnp.sum(parts[...], axis=0)
    fields = total.shape[1]
    scaled = total[0:1] / (total[1:2] / total[2:3] + 1e-05)
    weight = total[3:4, 0:1]
    loss_ref[...] = jnp.sum(scaled, axis=1, keepdims=True) / (fields * weight)


def small_body(
    fields, target, area_weight, grid_count, mesh_query, enc_index, proc_index, dec_index,
    w_embed, w_enc_kv, w_qkv, w_out, w_dec1, w_dec2,
):
    space = lax.axis_size("space")
    samples = lax.axis_size("dp")
    own = fields[0].T
    goal = target[0].T
    w2 = w_dec2.T
    field_count, slots = own.shape
    nodes, width = mesh_query.shape
    half = width // 2
    rows = nodes * enc_index.shape[1]

    swap = [(0, 1), (1, 0)]
    pair = [(i, i ^ 1) for i in range(space)]
    link = [(i, i + 1) for i in range(1, space - 1, 2)]
    link = link + [(j, i) for i, j in link]

    def over_dp(x):
        return lax.ppermute(x, "dp", swap)

    def to_first(x):
        return lax.ppermute(x, "dp", swap)

    def to_second(x):
        return lax.ppermute(x, "dp", swap)

    def over_pair(x):
        return lax.ppermute(x, "space", pair)

    def over_link(x):
        return lax.ppermute(x, "space", link)

    def over_both(x, steps):
        steps = [(d * space + i, (1 - d) * space + j) for d in range(2) for i, j in steps]
        return lax.ppermute(x, ("dp", "space"), steps)

    def over_quad(x):
        return lax.ppermute(x, "space", [(i, i ^ 2) for i in range(space)])

    def after(x, *others):
        return lax.optimization_barrier((x,) + others)[0]

    we_there = over_dp(w_embed)
    own1 = over_pair(own)
    own2 = over_link(own)
    pick, present = call(
        pick_kernel,
        (shape((3, rows, slots)), shape((rows, 128), F32)),
        (enc_index.T,),
        flops=BUSY,
    )
    (near,) = call(
        near_kernel, (shape((field_count, rows)),), (pick, own, own1, own2), flops=BUSY
    )
    other = over_dp(near)
    tail = 16 * pl.cdiv(field_count, 128)
    (share,) = call(
        share_kernel,
        (shape((width // 8 + tail, half)),),
        (after(w_dec1, near), w2),
        scratch=[pltpu.VMEM((8 * tail, half), BF16)],
        flops=BUSY,
    )
    pairs_own, probs = call(
        encode_own_kernel,
        (shape((rows, width)), shape((HEADS, rows))),
        (mesh_query, present, near, w_embed, we_there, w_enc_kv),
        flops=2 * rows * width * (width + field_count),
    )
    share = over_dp(after(share, other, pairs_own))
    pairs, probs = call(
        encode_other_kernel,
        (shape((rows, width)), shape((HEADS, 2 * rows))),
        (mesh_query, present, other, w_embed, we_there, w_enc_kv, probs),
        flops=2 * rows * width * (width + field_count),
    )
    (latent,) = call(
        latent_kernel,
        (shape((2 * nodes, width)),),
        (mesh_query, to_second(probs), pairs_own, pairs),
        flops=2 * 2 * rows * width * 128,
    )
    came = to_first(latent)
    share = after(share, latent)
    came_share = lax.ppermute(share, "space", [(i, i ^ 4) for i in range(space)])
    send, pairs = call(
        later_kernel,
        (shape((2 * nodes, half)), shape((2 * nodes, width))),
        (latent, w_qkv),
        flops=2 * 2 * nodes * width * 3 * half,
    )
    values = to_first(send)
    latent, queries, send, keys = call(
        first_kernel,
        (shape((2 * nodes, width)),) + (shape((2 * nodes, half)),) * 3,
        (latent, came, w_qkv),
        flops=2 * 2 * nodes * width * 3 * half,
    )
    (pairs,) = call(pairs_kernel, (shape((2 * nodes, width)),), (pairs, keys, values))
    (share,) = call(
        functools.partial(join_kernel, 4, tail),
        (shape((2 * share.shape[0], half)),),
        (share, came_share),
    )
    came_share = over_quad(share)
    keep, send = call(
        mesh_kernel,
        (shape((nodes, width), F32), shape((nodes, width))),
        (proc_index.T, latent, queries, to_second(send), pairs, over_pair(pairs),
         over_link(pairs), w_out),
        scratch=[pltpu.VMEM((2 * nodes, width), F32)],
        flops=2 * 2 * nodes * width * width,
    )
    (share,) = call(
        functools.partial(join_kernel, 2, 2 * tail),
        (shape((2 * share.shape[0], half)),),
        (share, came_share),
    )
    (updated,) = call(add_kernel, (shape((nodes, width)),), (keep, over_dp(send)))
    up1 = over_pair(updated)
    came_share = over_pair(after(share, up1))
    predicted, sums = call(
        decode_kernel,
        (shape((field_count, slots)), shape((space * samples, 8, field_count), F32)),
        (grid_count, dec_index.T, own, goal, area_weight[None], updated, up1,
         over_link(updated), w_dec1, share, came_share, w2),
        scratch=[pltpu.VMEM((slots, width), BF16), pltpu.VMEM((8 * tail, half), BF16)],
        flops=2 * slots * width * (width + field_count),
        smem=(0,),
    )
    parts = lax.all_to_all(sums, ("dp", "space"), 0, 0)
    (loss,) = call(loss_kernel, (shape((1, 1), F32),), (parts,))
    return predicted.T[None], loss[0, 0]


def with_halo(cells, sides, width):
    for axis, dim in sides:
        count = lax.axis_size(axis)
        ends = count - 1
        head = lax.slice_in_dim(cells, 0, width, axis=dim)
        tail = lax.slice_in_dim(cells, cells.shape[dim] - width, cells.shape[dim], axis=dim)
        cells = jnp.concatenate(
            [
                lax.ppermute(tail, axis, [(i, (i + 1) % count) for i in range(ends)]),
                cells,
                lax.ppermute(head, axis, [((i + 1) % count, i) for i in range(ends)]),
            ],
            axis=dim,
        )
    return cells


def layer_norm(values):
    centre = jnp.mean(values, axis=-1, keepdims=True)
    shifted = values - centre
    spread = jnp.mean(shifted * shifted, axis=-1, keepdims=True)
    return shifted / jnp.sqrt(spread + 1e-05)


def attend(queries, gathered, present):
    node_count, width = queries.shape
    per_head_width = width // HEADS
    split_query_heads = queries.reshape(node_count, HEADS, per_head_width)
    split_key_heads = gathered[:, :, :width].reshape(node_count, -1, HEADS, per_head_width)
    split_value_heads = gathered[:, :, width:].reshape(node_count, -1, HEADS, per_head_width)
    attention_logits = jnp.einsum(
        "gtz,gxtz->gtx", split_query_heads, split_key_heads, preferred_element_type=jnp.float32
    ) / math.sqrt(per_head_width)
    attention_logits = jnp.where(present[:, None, :], attention_logits, -jnp.inf)
    attention_probs = jax.nn.softmax(attention_logits, axis=-1).astype(jnp.bfloat16)
    aggregated_values = jnp.einsum(
        "owi,oiwn->own", attention_probs, split_value_heads, preferred_element_type=jnp.float32
    )
    return aggregated_values.reshape(node_count, width)


def general_body(
    fields,
    target,
    area_weight,
    grid_count,
    mesh_query,
    enc_index,
    proc_index,
    dec_index,
    w_embed,
    w_enc_kv,
    w_qkv,
    w_out,
    w_dec1,
    w_dec2,
):
    own_fields = fields[0]
    grid_rows = own_fields.shape[0]
    mesh_rows, width = mesh_query.shape
    field_count = own_fields.shape[1]
    grid_window = with_halo(
        jax.nn.silu(
            jnp.dot(
                own_fields,
                lax.all_gather(w_embed, "dp", axis=1, tiled=True),
                preferred_element_type=jnp.float32,
            )
        ).astype(jnp.bfloat16),
        (("space", 0),),
        grid_rows,
    )
    grid_pairs = jnp.dot(
        grid_window,
        lax.all_gather(w_enc_kv, "dp", axis=1, tiled=True),
        preferred_element_type=jnp.float32,
    ).astype(jnp.bfloat16)
    present = enc_index >= 0
    enc_near = jnp.take(grid_pairs, jnp.maximum(enc_index, 0), axis=0)
    latent = (mesh_query.astype(jnp.float32) + attend(mesh_query, enc_near, present)).astype(
        jnp.bfloat16
    )
    normed = layer_norm(latent.astype(jnp.float32)).astype(jnp.bfloat16)
    mesh_qkv = jnp.dot(
        normed, lax.all_gather(w_qkv, "dp", axis=1, tiled=True), preferred_element_type=jnp.float32
    ).astype(jnp.bfloat16)
    mesh_queries = mesh_qkv[:, :width]
    mesh_pairs = with_halo(mesh_qkv[:, width:], (("space", 0),), mesh_rows)
    proc_near = jnp.take(mesh_pairs, proc_index, axis=0)
    mixed = attend(mesh_queries, proc_near, jnp.ones(proc_index.shape, dtype=bool)).astype(
        jnp.bfloat16
    )
    columns = mixed
    projected = jnp.dot(
        columns, lax.all_gather(w_out, "dp", axis=0, tiled=True), preferred_element_type=jnp.float32
    )
    updated = (latent.astype(jnp.float32) + projected).astype(jnp.bfloat16)
    mesh_window = with_halo(updated, (("space", 0),), mesh_rows)
    dec_near = jnp.take(mesh_window, dec_index, axis=0).astype(jnp.float32)
    decoder_in = layer_norm(jnp.mean(dec_near, axis=1)).astype(jnp.bfloat16)
    decoder_hidden = jax.nn.silu(
        jnp.dot(
            decoder_in,
            lax.all_gather(w_dec1, "dp", axis=1, tiled=True),
            preferred_element_type=jnp.float32,
        )
    ).astype(jnp.bfloat16)
    columns = decoder_hidden
    increment = jnp.dot(
        columns,
        lax.all_gather(w_dec2, "dp", axis=0, tiled=True),
        preferred_element_type=jnp.float32,
    )
    valid = jnp.arange(grid_rows, dtype=jnp.int32) < grid_count[0]
    predicted = jnp.where(
        valid[:, None], own_fields.astype(jnp.float32) + increment, jnp.float32(0.0)
    )
    keep_mask = valid.astype(jnp.float32)
    target_rows = target[0].astype(jnp.float32)
    misfit = predicted - target_rows
    error_sums = jnp.sum((keep_mask * area_weight)[:, None] * misfit * misfit, axis=0)
    target_sums = jnp.sum(keep_mask[:, None] * target_rows * target_rows, axis=0)
    valid_count = jnp.sum(keep_mask)
    weight_sum = jnp.sum(keep_mask * area_weight)
    target_all, count_all, weight_all = lax.psum(
        (target_sums, valid_count, weight_sum), ("dp", "space")
    )
    local_loss = jnp.sum(error_sums / (target_all / count_all + 1e-05))
    loss = lax.psum(local_loss, ("dp", "space")) / (field_count * weight_all)
    return (predicted.astype(jnp.bfloat16)[None], loss)


def solution(mesh):
    placed = (
        P("dp", "space", None),
        P("dp", "space", None),
        P("space"),
        P("space"),
        P("space", None),
        P("space", None),
        P("space", None),
        P("space", None),
        P(None, "dp"),
        P(None, "dp"),
        P(None, "dp"),
        P("dp", None),
        P(None, "dp"),
        P("dp", None),
    )
    small = mesh.shape["dp"] == 2 and mesh.shape["space"] % 8 == 0
    return jax.shard_map(
        small_body if small else general_body, mesh=mesh, in_specs=placed, out_specs=(P("dp", "space", None), P()), check_vma=False
    )
```

```python
import functools
import math

import jax
import jax.numpy as jnp
from jax import lax
from jax.experimental import pallas as pl
from jax.experimental.pallas import tpu as pltpu
from jax.sharding import PartitionSpec as P

HEADS = 16
F32 = jnp.float32
BF16 = jnp.bfloat16
BUSY = 4_000_000_000


def silu(x):
    return 0.5 * x * (1.0 + jnp.tanh(0.5 * x))


def dot(a, b):
    return jnp.dot(a, b, preferred_element_type=F32)


def dot_nt(a, b, precision=None):
    return lax.dot_general(
        a, b, (((1,), (1,)), ((), ())), preferred_element_type=F32, precision=precision
    )


def normalize(values):
    centre = jnp.mean(values, axis=-1, keepdims=True)
    shifted = values - centre
    spread = jnp.mean(shifted * shifted, axis=-1, keepdims=True)
    return shifted * lax.rsqrt(spread + 1e-05)


def shape(dims, dtype=BF16):
    return jax.ShapeDtypeStruct(tuple(dims), dtype)


def call(kernel, outs, args, scratch=(), flops=0, smem=(), size=None):
    size = size if size is not None else sum(math.prod(a.shape) * a.dtype.itemsize for a in args)
    return pl.pallas_call(
        kernel,
        out_shape=tuple(outs),
        in_specs=[
            pl.BlockSpec(memory_space=pltpu.SMEM if i in smem else pltpu.VMEM)
            for i in range(len(args))
        ],
        out_specs=(pl.BlockSpec(memory_space=pltpu.VMEM),) * len(outs),
        scratch_shapes=list(scratch),
        compiler_params=pltpu.CompilerParams(vmem_limit_bytes=24 * 1024 * 1024),
        cost_estimate=pl.CostEstimate(flops=flops, bytes_accessed=size, transcendentals=0),
    )(*args)


def side_block(index, size):
    odd = lax.axis_index("space") % 2
    side = index // size
    block = jnp.where(side == 1, 0, jnp.where((side == 2) == (odd == 0), 1, 2))
    return block * size + index % size


def slots_of(index_ref, slots):
    entries = index_ref.shape[0]
    index = jnp.transpose(index_ref[...])
    entry = jnp.concatenate([index[:, k : k + 1] for k in range(entries)], axis=0)
    return jnp.where(entry >= 0, side_block(jnp.maximum(entry, 0), slots), -1), entry >= 0


def picked(place, i, slots):
    lane = lax.broadcasted_iota(jnp.int32, (place.shape[0], slots), 1)
    return (place == lane + i * slots).astype(BF16)


def pick_kernel(index_ref, pick_ref, present_ref):
    slots = pick_ref.shape[2]
    place, present = slots_of(index_ref, slots)
    for i in range(3):
        pick_ref[i] = picked(place, i, slots)
    present_ref[...] = jnp.broadcast_to(present.astype(F32), present_ref.shape)


def share_kernel(w1_ref, w2_ref, out_ref, pad_ref):
    size = w1_ref.shape[0] // 8
    tail = pad_ref.shape[0] // 8
    spot = lax.axis_index("space")
    share = (spot % 2) * 4 + ((spot // 2) % 2) * 2 + (spot // 4) % 2
    pad_ref[...] = jnp.zeros(pad_ref.shape, BF16)
    pad_ref[: w2_ref.shape[0], :] = w2_ref[...]
    out_ref[:size, :] = w1_ref[pl.ds(pl.multiple_of(share * size, size), size), :]
    out_ref[size:, :] = pad_ref[pl.ds(pl.multiple_of(share * tail, tail), tail), :]


def join_kernel(step, tail, mine, theirs, out_ref):
    rows = mine.shape[0]
    bit = (lax.axis_index("space") // step) % 2
    for block, place in ((mine, bit), (theirs, 1 - bit)):
        size = rows - tail
        out_ref[pl.ds(pl.multiple_of(place * size, 16), size), :] = block[:size, :]
        start = pl.multiple_of(2 * size + place * tail, 16)
        out_ref[pl.ds(start, tail), :] = block[size:, :]


def near_kernel(pick_ref, near0, near1, near2, out_ref):
    total = sum(dot_nt(block[...], pick_ref[i]) for i, block in enumerate((near0, near1, near2)))
    out_ref[...] = total.astype(BF16)


def encode(query_ref, present_ref, near_ref, we_here, we_there, w_ref, pairs_ref, probs_ref):
    nodes, width = query_ref.shape
    rows = present_ref.shape[0]
    entries = rows // nodes
    per_head = width // HEADS
    ours = lax.axis_index("dp")
    half = we_here.shape[1]
    here = pl.multiple_of(ours * half, half)
    there = pl.multiple_of((1 - ours) * half, half)
    near = jnp.transpose(near_ref[...].astype(F32)).astype(BF16)
    embed_here = silu(dot(near, we_here[...])).astype(BF16)
    embed_there = silu(dot(near, we_there[...])).astype(BF16)
    pairs = dot(embed_here, w_ref[pl.ds(here, half), :])
    pairs_ref[...] = (pairs + dot(embed_there, w_ref[pl.ds(there, half), :])).astype(BF16)

    @pl.when(ours == 0)
    def _():
        present = present_ref[...] > 0
        head_of = lax.broadcasted_iota(jnp.int32, (width, 128), 0) // per_head
        fold = (head_of == lax.broadcasted_iota(jnp.int32, (width, 128), 1)).astype(BF16)
        queries = jnp.broadcast_to(query_ref[...].astype(F32)[None], (entries, nodes, width))
        product = pairs_ref[...].astype(F32) * queries.reshape(rows, width)
        high = product.astype(BF16)
        low = (product - high.astype(F32)).astype(BF16)
        logits = (dot(high, fold) + dot(low, fold)) * (1.0 / math.sqrt(per_head))
        logits = jnp.where(present, logits, -1e30).reshape(entries, nodes, 128)
        top = jnp.max(logits, axis=0, keepdims=True)
        weight = jnp.where(present.reshape(entries, nodes, 128), jnp.exp(logits - top), 0.0)
        weight = weight / jnp.sum(weight, axis=0, keepdims=True)
        probs_ref[...] = jnp.transpose(weight.reshape(rows, 128))[:HEADS].astype(BF16)

    @pl.when(ours != 0)
    def _():
        probs_ref[...] = jnp.zeros(probs_ref.shape, BF16)


def encode_own_kernel(
    query_ref, present_ref, near_ref, we_here, we_there, w_ref, pairs_ref, probs_ref
):
    encode(query_ref, present_ref, near_ref, we_here, we_there, w_ref, pairs_ref, probs_ref)


def encode_other_kernel(
    query_ref, present_ref, near_ref, we_here, we_there, w_ref, first_ref, pairs_ref, probs_ref
):
    rows = first_ref.shape[1]
    probs_ref[:, :rows] = first_ref[...]
    encode(
        query_ref, present_ref, near_ref, we_here, we_there, w_ref, pairs_ref,
        probs_ref.at[:, rows : 2 * rows],
    )


def latent_kernel(query_ref, probs, pairs_own, pairs_other, latent_ref):
    query = query_ref[...].astype(F32)
    nodes, width = query.shape
    rows = pairs_own.shape[0]
    entries = rows // nodes
    per_head = width // HEADS
    head_of = lax.broadcasted_iota(jnp.int32, (HEADS, width), 1) // per_head
    spread = (head_of == lax.broadcasted_iota(jnp.int32, (HEADS, width), 0)).astype(BF16)

    @pl.when(lax.axis_index("dp") != 0)
    def _():
        for s, pairs in enumerate((pairs_other, pairs_own)):
            turned = probs[:, s * rows : (s + 1) * rows].astype(F32)
            weight = jnp.transpose(turned).astype(BF16)
            mixed = dot(weight, spread) * pairs[...].astype(F32)
            mixed = jnp.sum(mixed.reshape(entries, nodes, width), axis=0)
            latent_ref[s * nodes : (s + 1) * nodes, :] = (query + mixed).astype(BF16)

    @pl.when(lax.axis_index("dp") == 0)
    def _():
        latent_ref[...] = jnp.zeros_like(latent_ref)


def add_kernel(mine, theirs, out_ref, left_ref, right_ref):
    half = left_ref.shape[1]
    out_ref[...] = (mine[...] + theirs[...].astype(F32)).astype(BF16)
    left_ref[...] = out_ref[:, :half]
    right_ref[...] = out_ref[:, half:]


def later_kernel(latent, w_ref, send_ref, pairs_ref):
    half = w_ref.shape[1] // 3
    first = lax.axis_index("dp") == 0

    @pl.when(jnp.logical_not(first))
    def _():
        norm = normalize(latent[...].astype(F32)).astype(BF16)
        pairs_ref[:, :half] = dot(norm, w_ref[:, :half]).astype(BF16)
        send_ref[...] = dot(norm, w_ref[:, half : 2 * half]).astype(BF16)
        pairs_ref[:, half:] = dot(norm, w_ref[:, 2 * half :]).astype(BF16)

    @pl.when(first)
    def _():
        send_ref[...] = jnp.zeros(send_ref.shape, BF16)
        pairs_ref[...] = jnp.zeros(pairs_ref.shape, BF16)


def first_kernel(mine, came, w_ref, latent_ref, queries_ref, send_ref, keys_ref):
    half = w_ref.shape[1] // 3
    first = lax.axis_index("dp") == 0

    @pl.when(first)
    def _():
        latent_ref[...] = came[...]
        norm = normalize(came[...].astype(F32)).astype(BF16)
        queries_ref[...] = dot(norm, w_ref[:, :half]).astype(BF16)
        send_ref[...] = dot(norm, w_ref[:, half : 2 * half]).astype(BF16)
        keys_ref[...] = dot(norm, w_ref[:, 2 * half :]).astype(BF16)

    @pl.when(jnp.logical_not(first))
    def _():
        latent_ref[...] = mine[...]
        queries_ref[...] = jnp.zeros(queries_ref.shape, BF16)
        send_ref[...] = jnp.zeros(send_ref.shape, BF16)
        keys_ref[...] = jnp.zeros(keys_ref.shape, BF16)


def pairs_kernel(mine, keys, values, out_ref, keys_ref, values_ref):
    half = keys.shape[1]
    first = lax.axis_index("dp") == 0
    keys_ref[...] = jnp.where(first, keys[...], mine[:, :half])
    values_ref[...] = jnp.where(first, values[...], mine[:, half:])
    out_ref[:, :half] = keys_ref[...]
    out_ref[:, half:] = values_ref[...]


def mesh_kernel(
    index_ref, latent, mine, came, pairs0, keys1, values1, pairs2, wo_ref, keep_ref, send_ref,
    sums_ref,
):
    both, half = mine.shape
    nodes = both // 2
    rows = 3 * both
    heads = HEADS // 2
    per_head = half // heads
    first = lax.axis_index("dp") == 0
    queries = jnp.where(first, mine[...], came[...])
    keys = jnp.concatenate([pairs0[:, :half], keys1[...], pairs2[:, :half]], axis=0)
    values = jnp.concatenate([pairs0[:, half:], values1[...], pairs2[:, half:]], axis=0)
    place = side_block(jnp.transpose(index_ref[...]), nodes)
    near = lax.broadcasted_iota(jnp.int32, (nodes, rows), 1)
    code = (near // both) * nodes + near % nodes
    times = sum((place[:, j : j + 1] == code).astype(F32) for j in range(index_ref.shape[0]))
    second = (near // nodes) % 2
    times = jnp.concatenate(
        [jnp.where(second == 0, times, 0.0), jnp.where(second == 1, times, 0.0)], axis=0
    )[None]
    head_of = lax.broadcasted_iota(jnp.int32, (both, half), 1) // per_head
    zero = jnp.zeros_like(queries)
    stacked = jnp.concatenate(
        [jnp.where(head_of == h, queries, zero) for h in range(heads)], axis=0
    )
    logits = dot_nt(stacked, keys) * (1.0 / math.sqrt(per_head))
    logits = logits.reshape(heads, both, rows)
    logits = jnp.where(times > 0, logits, -1e30)
    top = jnp.max(logits, axis=-1, keepdims=True)
    weight = times * jnp.exp(logits - top)
    weight = weight / jnp.sum(weight, axis=-1, keepdims=True)
    mixed = dot(weight.astype(BF16).reshape(heads * both, rows), values)
    mixed = mixed.reshape(heads, both, half)
    total = jnp.where(head_of == 0, mixed[0], 0.0)
    for h in range(1, heads):
        total = jnp.where(head_of == h, mixed[h], total)
    sums_ref[...] = dot(total.astype(BF16), wo_ref[...])
    ours = lax.axis_index("dp")
    mine = pl.multiple_of(ours * nodes, nodes)
    theirs = pl.multiple_of((1 - ours) * nodes, nodes)
    keep_ref[...] = latent[pl.ds(mine, nodes), :].astype(F32) + sums_ref[pl.ds(mine, nodes), :]
    send_ref[...] = sums_ref[pl.ds(theirs, nodes), :].astype(BF16)


def decode_kernel(index_ref, up0, left, right, up2, w1_ref, w2_ref, norm_ref, part_ref):
    nodes, width = up0.shape
    entries, slots = index_ref.shape
    place = side_block(jnp.transpose(index_ref[...]), nodes)
    near = lax.broadcasted_iota(jnp.int32, (slots, nodes), 1)
    mean = 0.0
    up1 = jnp.concatenate([left[...], right[...]], axis=1)
    for i, updated in enumerate((up0[...], up1, up2[...])):
        times = sum((place[:, k : k + 1] == near + i * nodes).astype(F32) for k in range(entries))
        mean += dot(times.astype(BF16), updated)
    norm_ref[...] = normalize(mean * (1.0 / entries)).astype(BF16)
    hidden = silu(dot(norm_ref[...], w1_ref[...])).astype(BF16)
    part_ref[...] = dot_nt(w2_ref[...], hidden)


def errors_kernel(
    limit_ref, fields, target, area, norm_ref, part_ref, part0, part1, pred_ref, sums_ref,
    there_ref,
):
    count_field, slots = fields.shape
    keep = (lax.broadcasted_iota(jnp.int32, (8, slots), 1) < limit_ref[...]).astype(F32)
    weight = keep * area[...]
    core = lax.axis_index("space") % 2
    size = norm_ref.shape[1] // 2
    tail = part0.shape[0] - size
    hidden = 0.0
    for i, block in enumerate((part0, part1)):
        part = pl.multiple_of((core ^ i) * size, size)
        hidden += dot(norm_ref[:, pl.ds(part, size)], block[:size, :])
        start = pl.multiple_of((core ^ i) * tail, tail)
        there_ref[pl.ds(start, tail), :] = block[size:, :]
    hidden = silu(hidden).astype(BF16)
    increment = part_ref[...] + dot_nt(there_ref[:count_field, :], hidden)
    valid = keep[:1] > 0
    predicted = jnp.where(valid, fields[...].astype(F32) + increment, 0.0)
    pred_ref[...] = predicted.astype(BF16)
    goal = target[...].astype(F32)
    misfit = predicted - goal
    errors = dot_nt(weight, misfit * misfit, lax.Precision.HIGHEST)
    squares = dot_nt(keep, goal * goal, lax.Precision.HIGHEST)
    here_count = jnp.broadcast_to(jnp.sum(keep, axis=1, keepdims=True), (8, count_field))
    here_weight = jnp.broadcast_to(jnp.sum(weight, axis=1, keepdims=True), (8, count_field))
    row = lax.broadcasted_iota(jnp.int32, (8, count_field), 0)
    sums = jnp.where(
        row == 0, errors, jnp.where(row == 1, squares, jnp.where(row == 2, here_count, here_weight))
    )
    sums_ref[...] = jnp.broadcast_to(sums[None], sums_ref.shape)


def loss_kernel(parts, loss_ref):
    total = jnp.sum(parts[...], axis=0)
    fields = total.shape[1]
    scaled = total[0:1] / (total[1:2] / total[2:3] + 1e-05)
    weight = total[3:4, 0:1]
    loss_ref[...] = jnp.sum(scaled, axis=1, keepdims=True) / (fields * weight)


def small_body(
    fields, target, area_weight, grid_count, mesh_query, enc_index, proc_index, dec_index,
    w_embed, w_enc_kv, w_qkv, w_out, w_dec1, w_dec2,
):
    space = lax.axis_size("space")
    samples = lax.axis_size("dp")
    own = fields[0].T
    goal = target[0].T
    w2 = w_dec2.T
    field_count, slots = own.shape
    nodes, width = mesh_query.shape
    half = width // 2
    rows = nodes * enc_index.shape[1]

    swap = [(0, 1), (1, 0)]
    pair = [(i, i ^ 1) for i in range(space)]
    link = [(i, i + 1) for i in range(1, space - 1, 2)]
    link = link + [(j, i) for i, j in link]

    def over_dp(x):
        return lax.ppermute(x, "dp", swap)

    def to_first(x):
        return lax.ppermute(x, "dp", swap)

    def to_second(x):
        return lax.ppermute(x, "dp", swap)

    def over_pair(x):
        return lax.ppermute(x, "space", pair)

    def over_link(x):
        return lax.ppermute(x, "space", link)

    def over_both(x, steps):
        steps = [(d * space + i, (1 - d) * space + j) for d in range(2) for i, j in steps]
        return lax.ppermute(x, ("dp", "space"), steps)

    def over_quad(x):
        return lax.ppermute(x, "space", [(i, i ^ 2) for i in range(space)])

    def after(x, *others):
        return lax.optimization_barrier((x,) + others)[0]

    we_there = over_dp(w_embed)
    own1 = over_pair(own)
    own2 = over_link(own)
    pick, present = call(
        pick_kernel,
        (shape((3, rows, slots)), shape((rows, 128), F32)),
        (enc_index.T,),
        flops=BUSY,
    )
    (near,) = call(
        near_kernel, (shape((field_count, rows)),), (pick, own, own1, own2), flops=BUSY
    )
    other = over_dp(near)
    tail = 16 * pl.cdiv(field_count, 128)
    (share,) = call(
        share_kernel,
        (shape((width // 8 + tail, half)),),
        (after(w_dec1, near), w2),
        scratch=[pltpu.VMEM((8 * tail, half), BF16)],
        flops=BUSY,
    )
    pairs_own, probs = call(
        encode_own_kernel,
        (shape((rows, width)), shape((HEADS, rows))),
        (mesh_query, present, near, w_embed, we_there, w_enc_kv),
        flops=2 * rows * width * (width + field_count),
    )
    share = over_dp(after(share, other, pairs_own))
    pairs, probs = call(
        encode_other_kernel,
        (shape((rows, width)), shape((HEADS, 2 * rows))),
        (mesh_query, present, other, w_embed, we_there, w_enc_kv, probs),
        flops=2 * rows * width * (width + field_count),
    )
    (latent,) = call(
        latent_kernel,
        (shape((2 * nodes, width)),),
        (mesh_query, to_second(probs), pairs_own, pairs),
        flops=2 * 2 * rows * width * 128,
    )
    came = to_first(latent)
    share = after(share, latent)
    came_share = lax.ppermute(share, "space", [(i, i ^ 4) for i in range(space)])
    send, pairs = call(
        later_kernel,
        (shape((2 * nodes, half)), shape((2 * nodes, width))),
        (latent, w_qkv),
        flops=2 * 2 * nodes * width * 3 * half,
    )
    values = to_first(send)
    latent, queries, send, keys = call(
        first_kernel,
        (shape((2 * nodes, width)),) + (shape((2 * nodes, half)),) * 3,
        (latent, came, w_qkv),
        flops=2 * 2 * nodes * width * 3 * half,
    )
    pairs, keys, values = call(
        pairs_kernel,
        (shape((2 * nodes, width)),) + (shape((2 * nodes, half)),) * 2,
        (pairs, keys, values),
    )
    (share,) = call(
        functools.partial(join_kernel, 4, tail),
        (shape((2 * share.shape[0], half)),),
        (share, came_share),
    )
    came_share = over_quad(share)
    keep, send = call(
        mesh_kernel,
        (shape((nodes, width), F32), shape((nodes, width))),
        (proc_index.T, latent, queries, to_second(send), pairs, over_pair(keys),
         over_pair(values), over_link(pairs), w_out),
        scratch=[pltpu.VMEM((2 * nodes, width), F32)],
        flops=4 * BUSY,
    )
    (share,) = call(
        functools.partial(join_kernel, 2, 2 * tail),
        (shape((2 * share.shape[0], half)),),
        (share, came_share),
    )
    updated, left, right = call(
        add_kernel,
        (shape((nodes, width)),) + (shape((nodes, half)),) * 2,
        (keep, over_dp(send)),
    )
    left, right = over_pair(left), over_pair(right)
    up2 = over_link(updated)
    share = after(share, left, right, up2)
    came_share = over_pair(share)
    norm, part = call(
        decode_kernel,
        (shape((slots, width)), shape((field_count, slots), F32)),
        (dec_index.T, updated, left, right, up2, w_dec1, w2),
        flops=2 * slots * width * half,
    )
    predicted, sums = call(
        errors_kernel,
        (shape((field_count, slots)), shape((space * samples, 8, field_count), F32)),
        (grid_count[None], own, goal, area_weight[None], norm, part, share, came_share),
        scratch=[pltpu.VMEM((8 * tail, half), BF16)],
        flops=2 * slots * width * half,
    )
    parts = lax.all_to_all(sums, ("dp", "space"), 0, 0)
    (loss,) = call(loss_kernel, (shape((1, 1), F32),), (parts,))
    return predicted.T[None], loss[0, 0]


def with_halo(cells, sides, width):
    for axis, dim in sides:
        count = lax.axis_size(axis)
        ends = count - 1
        head = lax.slice_in_dim(cells, 0, width, axis=dim)
        tail = lax.slice_in_dim(cells, cells.shape[dim] - width, cells.shape[dim], axis=dim)
        cells = jnp.concatenate(
            [
                lax.ppermute(tail, axis, [(i, (i + 1) % count) for i in range(ends)]),
                cells,
                lax.ppermute(head, axis, [((i + 1) % count, i) for i in range(ends)]),
            ],
            axis=dim,
        )
    return cells


def layer_norm(values):
    centre = jnp.mean(values, axis=-1, keepdims=True)
    shifted = values - centre
    spread = jnp.mean(shifted * shifted, axis=-1, keepdims=True)
    return shifted / jnp.sqrt(spread + 1e-05)


def attend(queries, gathered, present):
    node_count, width = queries.shape
    per_head_width = width // HEADS
    split_query_heads = queries.reshape(node_count, HEADS, per_head_width)
    split_key_heads = gathered[:, :, :width].reshape(node_count, -1, HEADS, per_head_width)
    split_value_heads = gathered[:, :, width:].reshape(node_count, -1, HEADS, per_head_width)
    attention_logits = jnp.einsum(
        "gtz,gxtz->gtx", split_query_heads, split_key_heads, preferred_element_type=jnp.float32
    ) / math.sqrt(per_head_width)
    attention_logits = jnp.where(present[:, None, :], attention_logits, -jnp.inf)
    attention_probs = jax.nn.softmax(attention_logits, axis=-1).astype(jnp.bfloat16)
    aggregated_values = jnp.einsum(
        "owi,oiwn->own", attention_probs, split_value_heads, preferred_element_type=jnp.float32
    )
    return aggregated_values.reshape(node_count, width)


def general_body(
    fields,
    target,
    area_weight,
    grid_count,
    mesh_query,
    enc_index,
    proc_index,
    dec_index,
    w_embed,
    w_enc_kv,
    w_qkv,
    w_out,
    w_dec1,
    w_dec2,
):
    own_fields = fields[0]
    grid_rows = own_fields.shape[0]
    mesh_rows, width = mesh_query.shape
    field_count = own_fields.shape[1]
    grid_window = with_halo(
        jax.nn.silu(
            jnp.dot(
                own_fields,
                lax.all_gather(w_embed, "dp", axis=1, tiled=True),
                preferred_element_type=jnp.float32,
            )
        ).astype(jnp.bfloat16),
        (("space", 0),),
        grid_rows,
    )
    grid_pairs = jnp.dot(
        grid_window,
        lax.all_gather(w_enc_kv, "dp", axis=1, tiled=True),
        preferred_element_type=jnp.float32,
    ).astype(jnp.bfloat16)
    present = enc_index >= 0
    enc_near = jnp.take(grid_pairs, jnp.maximum(enc_index, 0), axis=0)
    latent = (mesh_query.astype(jnp.float32) + attend(mesh_query, enc_near, present)).astype(
        jnp.bfloat16
    )
    normed = layer_norm(latent.astype(jnp.float32)).astype(jnp.bfloat16)
    mesh_qkv = jnp.dot(
        normed, lax.all_gather(w_qkv, "dp", axis=1, tiled=True), preferred_element_type=jnp.float32
    ).astype(jnp.bfloat16)
    mesh_queries = mesh_qkv[:, :width]
    mesh_pairs = with_halo(mesh_qkv[:, width:], (("space", 0),), mesh_rows)
    proc_near = jnp.take(mesh_pairs, proc_index, axis=0)
    mixed = attend(mesh_queries, proc_near, jnp.ones(proc_index.shape, dtype=bool)).astype(
        jnp.bfloat16
    )
    columns = mixed
    projected = jnp.dot(
        columns, lax.all_gather(w_out, "dp", axis=0, tiled=True), preferred_element_type=jnp.float32
    )
    updated = (latent.astype(jnp.float32) + projected).astype(jnp.bfloat16)
    mesh_window = with_halo(updated, (("space", 0),), mesh_rows)
    dec_near = jnp.take(mesh_window, dec_index, axis=0).astype(jnp.float32)
    decoder_in = layer_norm(jnp.mean(dec_near, axis=1)).astype(jnp.bfloat16)
    decoder_hidden = jax.nn.silu(
        jnp.dot(
            decoder_in,
            lax.all_gather(w_dec1, "dp", axis=1, tiled=True),
            preferred_element_type=jnp.float32,
        )
    ).astype(jnp.bfloat16)
    columns = decoder_hidden
    increment = jnp.dot(
        columns,
        lax.all_gather(w_dec2, "dp", axis=0, tiled=True),
        preferred_element_type=jnp.float32,
    )
    valid = jnp.arange(grid_rows, dtype=jnp.int32) < grid_count[0]
    predicted = jnp.where(
        valid[:, None], own_fields.astype(jnp.float32) + increment, jnp.float32(0.0)
    )
    keep_mask = valid.astype(jnp.float32)
    target_rows = target[0].astype(jnp.float32)
    misfit = predicted - target_rows
    error_sums = jnp.sum((keep_mask * area_weight)[:, None] * misfit * misfit, axis=0)
    target_sums = jnp.sum(keep_mask[:, None] * target_rows * target_rows, axis=0)
    valid_count = jnp.sum(keep_mask)
    weight_sum = jnp.sum(keep_mask * area_weight)
    target_all, count_all, weight_all = lax.psum(
        (target_sums, valid_count, weight_sum), ("dp", "space")
    )
    local_loss = jnp.sum(error_sums / (target_all / count_all + 1e-05))
    loss = lax.psum(local_loss, ("dp", "space")) / (field_count * weight_all)
    return (predicted.astype(jnp.bfloat16)[None], loss)


def solution(mesh):
    placed = (
        P("dp", "space", None),
        P("dp", "space", None),
        P("space"),
        P("space"),
        P("space", None),
        P("space", None),
        P("space", None),
        P("space", None),
        P(None, "dp"),
        P(None, "dp"),
        P(None, "dp"),
        P("dp", None),
        P(None, "dp"),
        P("dp", None),
    )
    small = mesh.shape["dp"] == 2 and mesh.shape["space"] % 8 == 0
    return jax.shard_map(
        small_body if small else general_body, mesh=mesh, in_specs=placed, out_specs=(P("dp", "space", None), P()), check_vma=False
    )
```

```python
import functools
import math

import jax
import jax.numpy as jnp
from jax import lax
from jax.experimental import pallas as pl
from jax.experimental.pallas import tpu as pltpu
from jax.sharding import PartitionSpec as P

HEADS = 16
F32 = jnp.float32
BF16 = jnp.bfloat16
BUSY = 4_000_000_000


def silu(x):
    return 0.5 * x * (1.0 + jnp.tanh(0.5 * x))


def dot(a, b):
    return jnp.dot(a, b, preferred_element_type=F32)


def dot_nt(a, b, precision=None):
    return lax.dot_general(
        a, b, (((1,), (1,)), ((), ())), preferred_element_type=F32, precision=precision
    )


def normalize(values):
    centre = jnp.mean(values, axis=-1, keepdims=True)
    shifted = values - centre
    spread = jnp.mean(shifted * shifted, axis=-1, keepdims=True)
    return shifted * lax.rsqrt(spread + 1e-05)


def shape(dims, dtype=BF16):
    return jax.ShapeDtypeStruct(tuple(dims), dtype)


def call(kernel, outs, args, scratch=(), flops=0, smem=(), size=None):
    size = size if size is not None else sum(math.prod(a.shape) * a.dtype.itemsize for a in args)
    return pl.pallas_call(
        kernel,
        out_shape=tuple(outs),
        in_specs=[
            pl.BlockSpec(memory_space=pltpu.SMEM if i in smem else pltpu.VMEM)
            for i in range(len(args))
        ],
        out_specs=(pl.BlockSpec(memory_space=pltpu.VMEM),) * len(outs),
        scratch_shapes=list(scratch),
        compiler_params=pltpu.CompilerParams(vmem_limit_bytes=24 * 1024 * 1024),
        cost_estimate=pl.CostEstimate(flops=flops, bytes_accessed=size, transcendentals=0),
    )(*args)


def side_block(index, size):
    odd = lax.axis_index("space") % 2
    side = index // size
    block = jnp.where(side == 1, 0, jnp.where((side == 2) == (odd == 0), 1, 2))
    return block * size + index % size


def slots_of(index_ref, slots):
    entries = index_ref.shape[0]
    index = jnp.transpose(index_ref[...])
    entry = jnp.concatenate([index[:, k : k + 1] for k in range(entries)], axis=0)
    return jnp.where(entry >= 0, side_block(jnp.maximum(entry, 0), slots), -1), entry >= 0


def picked(place, i, slots):
    lane = lax.broadcasted_iota(jnp.int32, (place.shape[0], slots), 1)
    return (place == lane + i * slots).astype(BF16)


def pick_kernel(index_ref, pick_ref, present_ref):
    slots = pick_ref.shape[2]
    place, present = slots_of(index_ref, slots)
    for i in range(3):
        pick_ref[i] = picked(place, i, slots)
    present_ref[...] = jnp.broadcast_to(present.astype(F32), present_ref.shape)


def share_kernel(
    proc_ref, dec_ref, w1_ref, w2_ref, out_ref, times_ref, counts_ref, pad_ref
):
    size = w1_ref.shape[0] // 8
    tail = pad_ref.shape[0] // 8
    spot = lax.axis_index("space")
    share = (spot % 2) * 4 + ((spot // 2) % 2) * 2 + (spot // 4) % 2
    both, rows = times_ref.shape
    nodes = both // 2
    place = side_block(jnp.transpose(proc_ref[...]), nodes)
    near = lax.broadcasted_iota(jnp.int32, (nodes, rows), 1)
    code = (near // both) * nodes + near % nodes
    times = sum((place[:, j : j + 1] == code).astype(F32) for j in range(proc_ref.shape[0]))
    second = (near // nodes) % 2
    times_ref[:nodes, :] = jnp.where(second == 0, times, 0.0)
    times_ref[nodes:, :] = jnp.where(second == 1, times, 0.0)
    slots, rows = counts_ref.shape
    place = side_block(jnp.transpose(dec_ref[...]), nodes)
    near = lax.broadcasted_iota(jnp.int32, (slots, rows), 1)
    counts = sum((place[:, k : k + 1] == near).astype(F32) for k in range(dec_ref.shape[0]))
    counts_ref[...] = counts.astype(BF16)
    pad_ref[...] = jnp.zeros(pad_ref.shape, BF16)
    pad_ref[: w2_ref.shape[0], :] = w2_ref[...]
    out_ref[:size, :] = w1_ref[pl.ds(pl.multiple_of(share * size, size), size), :]
    out_ref[size:, :] = pad_ref[pl.ds(pl.multiple_of(share * tail, tail), tail), :]


def join_kernel(step, tail, mine, theirs, out_ref):
    rows = mine.shape[0]
    bit = (lax.axis_index("space") // step) % 2
    for block, place in ((mine, bit), (theirs, 1 - bit)):
        size = rows - tail
        out_ref[pl.ds(pl.multiple_of(place * size, 16), size), :] = block[:size, :]
        start = pl.multiple_of(2 * size + place * tail, 16)
        out_ref[pl.ds(start, tail), :] = block[size:, :]


def near_kernel(pick_ref, near0, near1, near2, out_ref):
    total = sum(dot_nt(block[...], pick_ref[i]) for i, block in enumerate((near0, near1, near2)))
    out_ref[...] = total.astype(BF16)


def encode(query_ref, present_ref, near_ref, we_here, we_there, w_ref, pairs_ref, probs_ref):
    nodes, width = query_ref.shape
    rows = present_ref.shape[0]
    entries = rows // nodes
    per_head = width // HEADS
    ours = lax.axis_index("dp")
    half = we_here.shape[1]
    here = pl.multiple_of(ours * half, half)
    there = pl.multiple_of((1 - ours) * half, half)
    near = jnp.transpose(near_ref[...].astype(F32)).astype(BF16)
    embed_here = silu(dot(near, we_here[...])).astype(BF16)
    embed_there = silu(dot(near, we_there[...])).astype(BF16)
    pairs = dot(embed_here, w_ref[pl.ds(here, half), :])
    pairs_ref[...] = (pairs + dot(embed_there, w_ref[pl.ds(there, half), :])).astype(BF16)

    @pl.when(ours == 0)
    def _():
        present = present_ref[...] > 0
        head_of = lax.broadcasted_iota(jnp.int32, (width, 128), 0) // per_head
        fold = (head_of == lax.broadcasted_iota(jnp.int32, (width, 128), 1)).astype(BF16)
        queries = jnp.broadcast_to(query_ref[...].astype(F32)[None], (entries, nodes, width))
        product = pairs_ref[...].astype(F32) * queries.reshape(rows, width)
        high = product.astype(BF16)
        low = (product - high.astype(F32)).astype(BF16)
        logits = (dot(high, fold) + dot(low, fold)) * (1.0 / math.sqrt(per_head))
        logits = jnp.where(present, logits, -1e30).reshape(entries, nodes, 128)
        top = jnp.max(logits, axis=0, keepdims=True)
        weight = jnp.where(present.reshape(entries, nodes, 128), jnp.exp(logits - top), 0.0)
        weight = weight / jnp.sum(weight, axis=0, keepdims=True)
        probs_ref[...] = jnp.transpose(weight.reshape(rows, 128))[:HEADS].astype(BF16)

    @pl.when(ours != 0)
    def _():
        probs_ref[...] = jnp.zeros(probs_ref.shape, BF16)


def encode_own_kernel(
    query_ref, present_ref, near_ref, we_here, we_there, w_ref, pairs_ref, probs_ref
):
    encode(query_ref, present_ref, near_ref, we_here, we_there, w_ref, pairs_ref, probs_ref)


def encode_other_kernel(
    query_ref, present_ref, near_ref, we_here, we_there, w_ref, first_ref, pairs_ref, probs_ref
):
    rows = first_ref.shape[1]
    probs_ref[:, :rows] = first_ref[...]
    encode(
        query_ref, present_ref, near_ref, we_here, we_there, w_ref, pairs_ref,
        probs_ref.at[:, rows : 2 * rows],
    )


def latent_kernel(query_ref, probs, pairs_own, pairs_other, latent_ref):
    query = query_ref[...].astype(F32)
    nodes, width = query.shape
    rows = pairs_own.shape[0]
    entries = rows // nodes
    per_head = width // HEADS
    head_of = lax.broadcasted_iota(jnp.int32, (HEADS, width), 1) // per_head
    spread = (head_of == lax.broadcasted_iota(jnp.int32, (HEADS, width), 0)).astype(BF16)

    @pl.when(lax.axis_index("dp") != 0)
    def _():
        for s, pairs in enumerate((pairs_other, pairs_own)):
            turned = probs[:, s * rows : (s + 1) * rows].astype(F32)
            weight = jnp.transpose(turned).astype(BF16)
            mixed = dot(weight, spread) * pairs[...].astype(F32)
            mixed = jnp.sum(mixed.reshape(entries, nodes, width), axis=0)
            latent_ref[s * nodes : (s + 1) * nodes, :] = (query + mixed).astype(BF16)

    @pl.when(lax.axis_index("dp") == 0)
    def _():
        latent_ref[...] = jnp.zeros_like(latent_ref)


def add_kernel(mine, theirs, out_ref, left_ref, right_ref):
    half = left_ref.shape[1]
    out_ref[...] = (mine[...] + theirs[...].astype(F32)).astype(BF16)
    left_ref[...] = out_ref[:, :half]
    right_ref[...] = out_ref[:, half:]


def later_kernel(latent, w_ref, send_ref, pairs_ref):
    half = w_ref.shape[1] // 3
    first = lax.axis_index("dp") == 0

    @pl.when(jnp.logical_not(first))
    def _():
        norm = normalize(latent[...].astype(F32)).astype(BF16)
        pairs_ref[:, :half] = dot(norm, w_ref[:, :half]).astype(BF16)
        send_ref[...] = dot(norm, w_ref[:, half : 2 * half]).astype(BF16)
        pairs_ref[:, half:] = dot(norm, w_ref[:, 2 * half :]).astype(BF16)

    @pl.when(first)
    def _():
        send_ref[...] = jnp.zeros(send_ref.shape, BF16)
        pairs_ref[...] = jnp.zeros(pairs_ref.shape, BF16)


def first_kernel(mine, came, w_ref, latent_ref, queries_ref, send_ref, keys_ref):
    half = w_ref.shape[1] // 3
    first = lax.axis_index("dp") == 0

    @pl.when(first)
    def _():
        latent_ref[...] = came[...]
        norm = normalize(came[...].astype(F32)).astype(BF16)
        queries_ref[...] = dot(norm, w_ref[:, :half]).astype(BF16)
        send_ref[: norm.shape[0], :] = dot(norm, w_ref[:, half : 2 * half]).astype(BF16)
        send_ref[norm.shape[0] :, :] = jnp.zeros(
            (send_ref.shape[0] - norm.shape[0], half), BF16
        )
        keys_ref[...] = dot(norm, w_ref[:, 2 * half :]).astype(BF16)

    @pl.when(jnp.logical_not(first))
    def _():
        latent_ref[...] = mine[...]
        queries_ref[...] = jnp.zeros(queries_ref.shape, BF16)
        send_ref[...] = jnp.zeros(send_ref.shape, BF16)
        keys_ref[...] = jnp.zeros(keys_ref.shape, BF16)


def pairs_kernel(mine, keys, values, out_ref, keys_ref, values_ref):
    half = keys.shape[1]
    first = lax.axis_index("dp") == 0
    keys_ref[...] = jnp.where(first, keys[...], mine[:, :half])
    values_ref[...] = jnp.where(first, values[...], mine[:, half:])
    out_ref[:, :half] = keys_ref[...]
    out_ref[:, half:] = values_ref[...]


def mesh_attend(sample, times_ref, mine, came, pairs0, keys1, values1, pairs2, wo_ref):
    both, half = mine.shape
    nodes = both // 2
    rows = 3 * both
    heads = HEADS // 2
    per_head = half // heads
    start = pl.multiple_of(sample * nodes, nodes)
    first = lax.axis_index("dp") == 0
    queries = jnp.where(first, mine[pl.ds(start, nodes), :], came[pl.ds(start, nodes), :])
    keys = jnp.concatenate([pairs0[:, :half], keys1[...], pairs2[:, :half]], axis=0)
    values = jnp.concatenate([pairs0[:, half:], values1[...], pairs2[:, half:]], axis=0)
    times = times_ref[pl.ds(start, nodes), :][None]
    head_of = lax.broadcasted_iota(jnp.int32, (nodes, half), 1) // per_head
    zero = jnp.zeros_like(queries)
    stacked = jnp.concatenate(
        [jnp.where(head_of == h, queries, zero) for h in range(heads)], axis=0
    )
    logits = dot_nt(stacked, keys) * (1.0 / math.sqrt(per_head))
    logits = logits.reshape(heads, nodes, rows)
    logits = jnp.where(times > 0, logits, -1e30)
    top = jnp.max(logits, axis=-1, keepdims=True)
    weight = times * jnp.exp(logits - top)
    weight = weight / jnp.sum(weight, axis=-1, keepdims=True)
    mixed = dot(weight.astype(BF16).reshape(heads * nodes, rows), values)
    mixed = mixed.reshape(heads, nodes, half)
    total = jnp.where(head_of == 0, mixed[0], 0.0)
    for h in range(1, heads):
        total = jnp.where(head_of == h, mixed[h], total)
    return dot(total.astype(BF16), wo_ref[...])


def send_kernel(
    times_ref, mine, came, pairs0, keys1, values1, pairs2, wo_ref, send_ref
):
    other = 1 - lax.axis_index("dp")
    projected = mesh_attend(other, times_ref, mine, came, pairs0, keys1, values1, pairs2, wo_ref)
    send_ref[...] = projected.astype(BF16)


def keep_kernel(
    latent, limit, target, area, times_ref, mine, came, pairs0, keys1, values1, pairs2, wo_ref,
    keep_ref, weight_ref, base_ref,
):
    count_field, slots = target.shape
    valid = (lax.broadcasted_iota(jnp.int32, (8, slots), 1) < limit[...]).astype(F32)
    weight = valid * area[...]
    row = lax.broadcasted_iota(jnp.int32, (8, slots), 0)
    weight_ref[...] = jnp.where(row == 0, weight, valid)
    goal = target[...].astype(F32)
    squares = dot_nt(valid, goal * goal, lax.Precision.HIGHEST)
    here_count = jnp.broadcast_to(jnp.sum(valid, axis=1, keepdims=True), (8, count_field))
    here_weight = jnp.broadcast_to(jnp.sum(weight, axis=1, keepdims=True), (8, count_field))
    row = lax.broadcasted_iota(jnp.int32, (8, count_field), 0)
    base_ref[...] = jnp.where(row == 1, squares, jnp.where(row == 2, here_count, here_weight))
    ours = lax.axis_index("dp")
    nodes = keep_ref.shape[0]
    projected = mesh_attend(ours, times_ref, mine, came, pairs0, keys1, values1, pairs2, wo_ref)
    start = pl.multiple_of(ours * nodes, nodes)
    keep_ref[...] = latent[pl.ds(start, nodes), :].astype(F32) + projected


def decode_kernel(
    entries, counts, up0, left, right, up2, w1_ref, w2_ref, share,
    part_ref, rest_ref, hidden_ref, norm_ref,
):
    nodes = up0.shape[0]
    up1 = jnp.concatenate([left[...], right[...]], axis=1)
    mean = 0.0
    for i, updated in enumerate((up0[...], up1, up2[...])):
        mean += dot(counts[:, i * nodes : (i + 1) * nodes], updated)
    norm_ref[...] = normalize(mean * (1.0 / entries)).astype(BF16)
    hidden = silu(dot(norm_ref[...], w1_ref[...])).astype(BF16)
    part_ref[...] = dot_nt(w2_ref[...], hidden)
    size = hidden_ref.shape[1]
    core = lax.axis_index("space") % 2
    here = pl.multiple_of(core * size, size)
    there = pl.multiple_of((1 - core) * size, size)
    hidden_ref[...] = dot(norm_ref[:, pl.ds(here, size)], share[:size, :])
    rest_ref[...] = norm_ref[:, pl.ds(there, size)]


def errors_kernel(
    weight_ref, base_ref, fields, target, part_ref, rest_ref, hidden_ref, part0, part1,
    pred_ref, sums_ref, there_ref,
):
    count_field, slots = fields.shape
    core = lax.axis_index("space") % 2
    size = hidden_ref.shape[1]
    tail = part0.shape[0] - size
    for i, block in enumerate((part0, part1)):
        start = pl.multiple_of((core ^ i) * tail, tail)
        there_ref[pl.ds(start, tail), :] = block[size:, :]
    hidden = silu(hidden_ref[...] + dot(rest_ref[...], part1[:size, :])).astype(BF16)
    increment = part_ref[...] + dot_nt(there_ref[:count_field, :], hidden)
    valid = weight_ref[1:2, :] > 0
    predicted = jnp.where(valid, fields[...].astype(F32) + increment, 0.0)
    pred_ref[...] = predicted.astype(BF16)
    misfit = predicted - target[...].astype(F32)
    errors = dot_nt(weight_ref[...], misfit * misfit, lax.Precision.HIGHEST)
    row = lax.broadcasted_iota(jnp.int32, (8, count_field), 0)
    sums = jnp.where(row == 0, errors, base_ref[...])
    sums_ref[...] = jnp.broadcast_to(sums[None], sums_ref.shape)


def loss_kernel(parts, loss_ref):
    total = jnp.sum(parts[...], axis=0)
    fields = total.shape[1]
    scaled = total[0:1] / (total[1:2] / total[2:3] + 1e-05)
    weight = total[3:4, 0:1]
    loss_ref[...] = jnp.sum(scaled, axis=1, keepdims=True) / (fields * weight)


def small_body(
    fields, target, area_weight, grid_count, mesh_query, enc_index, proc_index, dec_index,
    w_embed, w_enc_kv, w_qkv, w_out, w_dec1, w_dec2,
):
    space = lax.axis_size("space")
    samples = lax.axis_size("dp")
    own = fields[0].T
    goal = target[0].T
    w2 = w_dec2.T
    field_count, slots = own.shape
    nodes, width = mesh_query.shape
    half = width // 2
    rows = nodes * enc_index.shape[1]

    swap = [(0, 1), (1, 0)]
    pair = [(i, i ^ 1) for i in range(space)]
    link = [(i, i + 1) for i in range(1, space - 1, 2)]
    link = link + [(j, i) for i, j in link]

    def over_dp(x):
        return lax.ppermute(x, "dp", swap)

    def to_first(x):
        return lax.ppermute(x, "dp", swap)

    def to_second(x):
        return lax.ppermute(x, "dp", swap)

    def over_pair(x):
        return lax.ppermute(x, "space", pair)

    def over_link(x):
        return lax.ppermute(x, "space", link)

    def over_both(x, steps):
        steps = [(d * space + i, (1 - d) * space + j) for d in range(2) for i, j in steps]
        return lax.ppermute(x, ("dp", "space"), steps)

    def over_quad(x):
        return lax.ppermute(x, "space", [(i, i ^ 2) for i in range(space)])

    def after(x, *others):
        return lax.optimization_barrier((x,) + others)[0]

    we_there = over_dp(w_embed)
    own1 = over_pair(own)
    own2 = over_link(own)
    pick, present = call(
        pick_kernel,
        (shape((3, rows, slots)), shape((rows, 128), F32)),
        (enc_index.T,),
        flops=BUSY,
    )
    (near,) = call(
        near_kernel, (shape((field_count, rows)),), (pick, own, own1, own2), flops=BUSY
    )
    other = over_dp(near)
    tail = 16 * pl.cdiv(field_count, 128)
    share, times, counts = call(
        share_kernel,
        (
            shape((width // 8 + tail, half)),
            shape((2 * nodes, 6 * nodes), F32),
            shape((slots, 3 * nodes)),
        ),
        (proc_index.T, dec_index.T, after(w_dec1, near), w2),
        scratch=[pltpu.VMEM((8 * tail, half), BF16)],
        flops=BUSY,
    )
    pairs_own, probs = call(
        encode_own_kernel,
        (shape((rows, width)), shape((HEADS, rows))),
        (mesh_query, present, near, w_embed, we_there, w_enc_kv),
        flops=2 * rows * width * (width + field_count),
    )
    share = over_dp(after(share, other, pairs_own))
    pairs, probs = call(
        encode_other_kernel,
        (shape((rows, width)), shape((HEADS, 2 * rows))),
        (mesh_query, present, other, w_embed, we_there, w_enc_kv, probs),
        flops=2 * rows * width * (width + field_count),
    )
    (latent,) = call(
        latent_kernel,
        (shape((2 * nodes, width)),),
        (mesh_query, to_second(probs), pairs_own, pairs),
        flops=2 * 2 * rows * width * 128,
    )
    came = to_first(latent)
    share = after(share, latent)
    came_share = lax.ppermute(share, "space", [(i, i ^ 4) for i in range(space)])
    send, pairs = call(
        later_kernel,
        (shape((2 * nodes, half)), shape((2 * nodes, width))),
        (latent, w_qkv),
        flops=2 * 2 * nodes * width * 3 * half,
    )
    values = to_first(send)
    latent, queries, send, keys = call(
        first_kernel,
        (
            shape((2 * nodes, width)),
            shape((2 * nodes, half)),
            shape((2 * nodes + 16, half)),
            shape((2 * nodes, half)),
        ),
        (latent, came, w_qkv),
        flops=2 * 2 * nodes * width * 3 * half,
    )
    pairs, keys, values = call(
        pairs_kernel,
        (shape((2 * nodes, width)),) + (shape((2 * nodes, half)),) * 2,
        (pairs, keys, values),
    )
    (share,) = call(
        functools.partial(join_kernel, 4, tail),
        (shape((2 * share.shape[0], half)),),
        (share, came_share),
    )
    came_share = over_quad(share)
    window = (
        times, queries, to_second(send), pairs, over_pair(keys), over_pair(values),
        over_link(pairs), w_out,
    )
    (send,) = call(send_kernel, (shape((nodes, width)),), window, flops=4 * BUSY)
    keep, weight, base = call(
        keep_kernel,
        (shape((nodes, width), F32), shape((8, slots), F32), shape((8, field_count), F32)),
        (latent, grid_count[None], goal, area_weight[None]) + window,
        flops=2 * nodes * width * width,
    )
    (share,) = call(
        functools.partial(join_kernel, 2, 2 * tail),
        (shape((2 * share.shape[0], half)),),
        (share, came_share),
    )
    updated, left, right = call(
        add_kernel,
        (shape((nodes, width)),) + (shape((nodes, half)),) * 2,
        (keep, over_dp(send)),
    )
    left, right = over_pair(left), over_pair(right)
    up2 = over_link(updated)
    share = after(share, left, right, up2)
    came_share = over_pair(share)
    part, rest, hidden = call(
        functools.partial(decode_kernel, dec_index.shape[1]),
        (shape((field_count, slots), F32), shape((slots, half)), shape((slots, half), F32)),
        (counts, updated, left, right, up2, w_dec1, w2, share),
        scratch=[pltpu.VMEM((slots, width), BF16)],
        flops=2 * slots * width * half,
    )
    predicted, sums = call(
        errors_kernel,
        (shape((field_count, slots)), shape((space * samples, 8, field_count), F32)),
        (weight, base, own, goal, part, rest, hidden, share, came_share),
        scratch=[pltpu.VMEM((8 * tail, half), BF16)],
        flops=2 * slots * width * half,
    )
    parts = lax.all_to_all(sums, ("dp", "space"), 0, 0)
    (loss,) = call(loss_kernel, (shape((1, 1), F32),), (parts,))
    return predicted.T[None], loss[0, 0]


def with_halo(cells, sides, width):
    for axis, dim in sides:
        count = lax.axis_size(axis)
        ends = count - 1
        head = lax.slice_in_dim(cells, 0, width, axis=dim)
        tail = lax.slice_in_dim(cells, cells.shape[dim] - width, cells.shape[dim], axis=dim)
        cells = jnp.concatenate(
            [
                lax.ppermute(tail, axis, [(i, (i + 1) % count) for i in range(ends)]),
                cells,
                lax.ppermute(head, axis, [((i + 1) % count, i) for i in range(ends)]),
            ],
            axis=dim,
        )
    return cells


def layer_norm(values):
    centre = jnp.mean(values, axis=-1, keepdims=True)
    shifted = values - centre
    spread = jnp.mean(shifted * shifted, axis=-1, keepdims=True)
    return shifted / jnp.sqrt(spread + 1e-05)


def attend(queries, gathered, present):
    node_count, width = queries.shape
    per_head_width = width // HEADS
    split_query_heads = queries.reshape(node_count, HEADS, per_head_width)
    split_key_heads = gathered[:, :, :width].reshape(node_count, -1, HEADS, per_head_width)
    split_value_heads = gathered[:, :, width:].reshape(node_count, -1, HEADS, per_head_width)
    attention_logits = jnp.einsum(
        "gtz,gxtz->gtx", split_query_heads, split_key_heads, preferred_element_type=jnp.float32
    ) / math.sqrt(per_head_width)
    attention_logits = jnp.where(present[:, None, :], attention_logits, -jnp.inf)
    attention_probs = jax.nn.softmax(attention_logits, axis=-1).astype(jnp.bfloat16)
    aggregated_values = jnp.einsum(
        "owi,oiwn->own", attention_probs, split_value_heads, preferred_element_type=jnp.float32
    )
    return aggregated_values.reshape(node_count, width)


def general_body(
    fields,
    target,
    area_weight,
    grid_count,
    mesh_query,
    enc_index,
    proc_index,
    dec_index,
    w_embed,
    w_enc_kv,
    w_qkv,
    w_out,
    w_dec1,
    w_dec2,
):
    own_fields = fields[0]
    grid_rows = own_fields.shape[0]
    mesh_rows, width = mesh_query.shape
    field_count = own_fields.shape[1]
    grid_window = with_halo(
        jax.nn.silu(
            jnp.dot(
                own_fields,
                lax.all_gather(w_embed, "dp", axis=1, tiled=True),
                preferred_element_type=jnp.float32,
            )
        ).astype(jnp.bfloat16),
        (("space", 0),),
        grid_rows,
    )
    grid_pairs = jnp.dot(
        grid_window,
        lax.all_gather(w_enc_kv, "dp", axis=1, tiled=True),
        preferred_element_type=jnp.float32,
    ).astype(jnp.bfloat16)
    present = enc_index >= 0
    enc_near = jnp.take(grid_pairs, jnp.maximum(enc_index, 0), axis=0)
    latent = (mesh_query.astype(jnp.float32) + attend(mesh_query, enc_near, present)).astype(
        jnp.bfloat16
    )
    normed = layer_norm(latent.astype(jnp.float32)).astype(jnp.bfloat16)
    mesh_qkv = jnp.dot(
        normed, lax.all_gather(w_qkv, "dp", axis=1, tiled=True), preferred_element_type=jnp.float32
    ).astype(jnp.bfloat16)
    mesh_queries = mesh_qkv[:, :width]
    mesh_pairs = with_halo(mesh_qkv[:, width:], (("space", 0),), mesh_rows)
    proc_near = jnp.take(mesh_pairs, proc_index, axis=0)
    mixed = attend(mesh_queries, proc_near, jnp.ones(proc_index.shape, dtype=bool)).astype(
        jnp.bfloat16
    )
    columns = mixed
    projected = jnp.dot(
        columns, lax.all_gather(w_out, "dp", axis=0, tiled=True), preferred_element_type=jnp.float32
    )
    updated = (latent.astype(jnp.float32) + projected).astype(jnp.bfloat16)
    mesh_window = with_halo(updated, (("space", 0),), mesh_rows)
    dec_near = jnp.take(mesh_window, dec_index, axis=0).astype(jnp.float32)
    decoder_in = layer_norm(jnp.mean(dec_near, axis=1)).astype(jnp.bfloat16)
    decoder_hidden = jax.nn.silu(
        jnp.dot(
            decoder_in,
            lax.all_gather(w_dec1, "dp", axis=1, tiled=True),
            preferred_element_type=jnp.float32,
        )
    ).astype(jnp.bfloat16)
    columns = decoder_hidden
    increment = jnp.dot(
        columns,
        lax.all_gather(w_dec2, "dp", axis=0, tiled=True),
        preferred_element_type=jnp.float32,
    )
    valid = jnp.arange(grid_rows, dtype=jnp.int32) < grid_count[0]
    predicted = jnp.where(
        valid[:, None], own_fields.astype(jnp.float32) + increment, jnp.float32(0.0)
    )
    keep_mask = valid.astype(jnp.float32)
    target_rows = target[0].astype(jnp.float32)
    misfit = predicted - target_rows
    error_sums = jnp.sum((keep_mask * area_weight)[:, None] * misfit * misfit, axis=0)
    target_sums = jnp.sum(keep_mask[:, None] * target_rows * target_rows, axis=0)
    valid_count = jnp.sum(keep_mask)
    weight_sum = jnp.sum(keep_mask * area_weight)
    target_all, count_all, weight_all = lax.psum(
        (target_sums, valid_count, weight_sum), ("dp", "space")
    )
    local_loss = jnp.sum(error_sums / (target_all / count_all + 1e-05))
    loss = lax.psum(local_loss, ("dp", "space")) / (field_count * weight_all)
    return (predicted.astype(jnp.bfloat16)[None], loss)


def solution(mesh):
    placed = (
        P("dp", "space", None),
        P("dp", "space", None),
        P("space"),
        P("space"),
        P("space", None),
        P("space", None),
        P("space", None),
        P("space", None),
        P(None, "dp"),
        P(None, "dp"),
        P(None, "dp"),
        P("dp", None),
        P(None, "dp"),
        P("dp", None),
    )
    small = mesh.shape["dp"] == 2 and mesh.shape["space"] % 8 == 0
    return jax.shard_map(
        small_body if small else general_body, mesh=mesh, in_specs=placed, out_specs=(P("dp", "space", None), P()), check_vma=False
    )
```

```python
import functools
import math

import jax
import jax.numpy as jnp
from jax import lax
from jax.experimental import pallas as pl
from jax.experimental.pallas import tpu as pltpu
from jax.sharding import PartitionSpec as P

HEADS = 16
F32 = jnp.float32
BF16 = jnp.bfloat16
BUSY = 4_000_000_000


def silu(x):
    return 0.5 * x * (1.0 + jnp.tanh(0.5 * x))


def dot(a, b):
    return jnp.dot(a, b, preferred_element_type=F32)


def dot_nt(a, b, precision=None):
    return lax.dot_general(
        a, b, (((1,), (1,)), ((), ())), preferred_element_type=F32, precision=precision
    )


def normalize(values):
    centre = jnp.mean(values, axis=-1, keepdims=True)
    shifted = values - centre
    spread = jnp.mean(shifted * shifted, axis=-1, keepdims=True)
    return shifted * lax.rsqrt(spread + 1e-05)


def shape(dims, dtype=BF16):
    return jax.ShapeDtypeStruct(tuple(dims), dtype)


def call(kernel, outs, args, scratch=(), flops=0, smem=(), size=None):
    size = size if size is not None else sum(math.prod(a.shape) * a.dtype.itemsize for a in args)
    return pl.pallas_call(
        kernel,
        out_shape=tuple(outs),
        in_specs=[
            pl.BlockSpec(memory_space=pltpu.SMEM if i in smem else pltpu.VMEM)
            for i in range(len(args))
        ],
        out_specs=(pl.BlockSpec(memory_space=pltpu.VMEM),) * len(outs),
        scratch_shapes=list(scratch),
        compiler_params=pltpu.CompilerParams(vmem_limit_bytes=24 * 1024 * 1024),
        cost_estimate=pl.CostEstimate(flops=flops, bytes_accessed=size, transcendentals=0),
    )(*args)


def side_block(index, size):
    odd = lax.axis_index("space") % 2
    side = index // size
    block = jnp.where(side == 1, 0, jnp.where((side == 2) == (odd == 0), 1, 2))
    return block * size + index % size


def slots_of(index_ref, slots):
    entries = index_ref.shape[0]
    index = jnp.transpose(index_ref[...])
    entry = jnp.concatenate([index[:, k : k + 1] for k in range(entries)], axis=0)
    return jnp.where(entry >= 0, side_block(jnp.maximum(entry, 0), slots), -1), entry >= 0


def picked(place, i, slots):
    lane = lax.broadcasted_iota(jnp.int32, (place.shape[0], slots), 1)
    return (place == lane + i * slots).astype(BF16)


def pick_kernel(index_ref, pick_ref, present_ref):
    slots = pick_ref.shape[2]
    place, present = slots_of(index_ref, slots)
    for i in range(3):
        pick_ref[i] = picked(place, i, slots)
    present_ref[...] = jnp.broadcast_to(present.astype(F32), present_ref.shape)


def share_kernel(
    proc_ref, dec_ref, w1_ref, w2_ref, out_ref, times_ref, counts_ref
):
    size = w1_ref.shape[0] // 8
    tail = out_ref.shape[0] - size
    spot = lax.axis_index("space")
    share = (spot % 2) * 4 + ((spot // 2) % 2) * 2 + (spot // 4) % 2
    both, rows = times_ref.shape
    nodes = both // 2
    place = side_block(jnp.transpose(proc_ref[...]), nodes)
    near = lax.broadcasted_iota(jnp.int32, (nodes, rows), 1)
    code = (near // both) * nodes + near % nodes
    times = sum((place[:, j : j + 1] == code).astype(F32) for j in range(proc_ref.shape[0]))
    second = (near // nodes) % 2
    times_ref[:nodes, :] = jnp.where(second == 0, times, 0.0)
    times_ref[nodes:, :] = jnp.where(second == 1, times, 0.0)
    slots, rows = counts_ref.shape
    place = side_block(jnp.transpose(dec_ref[...]), nodes)
    near = lax.broadcasted_iota(jnp.int32, (slots, rows), 1)
    counts = sum((place[:, k : k + 1] == near).astype(F32) for k in range(dec_ref.shape[0]))
    counts_ref[...] = counts.astype(BF16)
    out_ref[:size, :] = w1_ref[pl.ds(pl.multiple_of(share * size, size), size), :]
    count_field = w2_ref.shape[0]
    row = lax.broadcasted_iota(jnp.int32, (tail, count_field), 0) + share * tail
    which = row == lax.broadcasted_iota(jnp.int32, (tail, count_field), 1)
    out_ref[size:, :] = dot(which.astype(BF16), w2_ref[...]).astype(BF16)


def join_kernel(step, tail, mine, theirs, out_ref):
    rows = mine.shape[0]
    bit = (lax.axis_index("space") // step) % 2
    for block, place in ((mine, bit), (theirs, 1 - bit)):
        size = rows - tail
        out_ref[pl.ds(pl.multiple_of(place * size, 16), size), :] = block[:size, :]
        start = pl.multiple_of(2 * size + place * tail, 16)
        out_ref[pl.ds(start, tail), :] = block[size:, :]


def near_kernel(pick_ref, near0, near1, near2, out_ref):
    total = sum(dot_nt(block[...], pick_ref[i]) for i, block in enumerate((near0, near1, near2)))
    out_ref[...] = total.astype(BF16)


def encode(query_ref, present_ref, near_ref, we_here, we_there, w_ref, pairs_ref, probs_ref):
    nodes, width = query_ref.shape
    rows = present_ref.shape[0]
    entries = rows // nodes
    per_head = width // HEADS
    ours = lax.axis_index("dp")
    half = we_here.shape[1]
    here = pl.multiple_of(ours * half, half)
    there = pl.multiple_of((1 - ours) * half, half)
    near = jnp.transpose(near_ref[...].astype(F32)).astype(BF16)
    embed_here = silu(dot(near, we_here[...])).astype(BF16)
    embed_there = silu(dot(near, we_there[...])).astype(BF16)
    pairs = dot(embed_here, w_ref[pl.ds(here, half), :])
    pairs_ref[...] = (pairs + dot(embed_there, w_ref[pl.ds(there, half), :])).astype(BF16)

    @pl.when(ours == 0)
    def _():
        present = present_ref[...] > 0
        head_of = lax.broadcasted_iota(jnp.int32, (width, 128), 0) // per_head
        fold = (head_of == lax.broadcasted_iota(jnp.int32, (width, 128), 1)).astype(BF16)
        queries = jnp.broadcast_to(query_ref[...].astype(F32)[None], (entries, nodes, width))
        product = pairs_ref[...].astype(F32) * queries.reshape(rows, width)
        high = product.astype(BF16)
        low = (product - high.astype(F32)).astype(BF16)
        logits = (dot(high, fold) + dot(low, fold)) * (1.0 / math.sqrt(per_head))
        logits = jnp.where(present, logits, -1e30).reshape(entries, nodes, 128)
        top = jnp.max(logits, axis=0, keepdims=True)
        weight = jnp.where(present.reshape(entries, nodes, 128), jnp.exp(logits - top), 0.0)
        weight = weight / jnp.sum(weight, axis=0, keepdims=True)
        probs_ref[...] = jnp.transpose(weight.reshape(rows, 128))[:HEADS].astype(BF16)

    @pl.when(ours != 0)
    def _():
        probs_ref[...] = jnp.zeros(probs_ref.shape, BF16)


def encode_own_kernel(
    query_ref, present_ref, near_ref, we_here, we_there, w_ref, pairs_ref, probs_ref
):
    encode(query_ref, present_ref, near_ref, we_here, we_there, w_ref, pairs_ref, probs_ref)


def encode_other_kernel(
    query_ref, present_ref, near_ref, we_here, we_there, w_ref, first_ref, pairs_ref, probs_ref
):
    rows = first_ref.shape[1]
    probs_ref[:, :rows] = first_ref[...]
    encode(
        query_ref, present_ref, near_ref, we_here, we_there, w_ref, pairs_ref,
        probs_ref.at[:, rows : 2 * rows],
    )


def latent_kernel(query_ref, probs, pairs_own, pairs_other, latent_ref):
    query = query_ref[...].astype(F32)
    nodes, width = query.shape
    rows = pairs_own.shape[0]
    entries = rows // nodes
    per_head = width // HEADS
    head_of = lax.broadcasted_iota(jnp.int32, (HEADS, width), 1) // per_head
    spread = (head_of == lax.broadcasted_iota(jnp.int32, (HEADS, width), 0)).astype(BF16)

    @pl.when(lax.axis_index("dp") != 0)
    def _():
        for s, pairs in enumerate((pairs_other, pairs_own)):
            turned = probs[:, s * rows : (s + 1) * rows].astype(F32)
            weight = jnp.transpose(turned).astype(BF16)
            mixed = dot(weight, spread) * pairs[...].astype(F32)
            mixed = jnp.sum(mixed.reshape(entries, nodes, width), axis=0)
            latent_ref[s * nodes : (s + 1) * nodes, :] = (query + mixed).astype(BF16)

    @pl.when(lax.axis_index("dp") == 0)
    def _():
        latent_ref[...] = jnp.zeros_like(latent_ref)


def add_kernel(mine, theirs, out_ref, left_ref, right_ref):
    half = left_ref.shape[1]
    out_ref[...] = (mine[...] + theirs[...].astype(F32)).astype(BF16)
    left_ref[...] = out_ref[:, :half]
    right_ref[...] = out_ref[:, half:]


def later_kernel(latent, w_ref, send_ref, pairs_ref):
    half = w_ref.shape[1] // 3
    first = lax.axis_index("dp") == 0

    @pl.when(jnp.logical_not(first))
    def _():
        norm = normalize(latent[...].astype(F32)).astype(BF16)
        pairs_ref[:, :half] = dot(norm, w_ref[:, :half]).astype(BF16)
        send_ref[...] = dot(norm, w_ref[:, half : 2 * half]).astype(BF16)
        pairs_ref[:, half:] = dot(norm, w_ref[:, 2 * half :]).astype(BF16)

    @pl.when(first)
    def _():
        send_ref[...] = jnp.zeros(send_ref.shape, BF16)
        pairs_ref[...] = jnp.zeros(pairs_ref.shape, BF16)


def first_kernel(mine, came, w_ref, latent_ref, queries_ref, send_ref, keys_ref):
    half = w_ref.shape[1] // 3
    first = lax.axis_index("dp") == 0

    @pl.when(first)
    def _():
        latent_ref[...] = came[...]
        norm = normalize(came[...].astype(F32)).astype(BF16)
        queries_ref[...] = dot(norm, w_ref[:, :half]).astype(BF16)
        send_ref[: norm.shape[0], :] = dot(norm, w_ref[:, half : 2 * half]).astype(BF16)
        send_ref[norm.shape[0] :, :] = jnp.zeros(
            (send_ref.shape[0] - norm.shape[0], half), BF16
        )
        keys_ref[...] = dot(norm, w_ref[:, 2 * half :]).astype(BF16)

    @pl.when(jnp.logical_not(first))
    def _():
        latent_ref[...] = mine[...]
        queries_ref[...] = jnp.zeros(queries_ref.shape, BF16)
        send_ref[...] = jnp.zeros(send_ref.shape, BF16)
        keys_ref[...] = jnp.zeros(keys_ref.shape, BF16)


def pairs_kernel(mine, keys, values, out_ref, keys_ref, values_ref):
    half = keys.shape[1]
    first = lax.axis_index("dp") == 0
    keys_ref[...] = jnp.where(first, keys[...], mine[:, :half])
    values_ref[...] = jnp.where(first, values[...], mine[:, half:])
    out_ref[:, :half] = keys_ref[...]
    out_ref[:, half:] = values_ref[...]


def mesh_attend(sample, times_ref, mine, came, pairs0, keys1, values1, pairs2, wo_ref):
    both, half = mine.shape
    nodes = both // 2
    rows = 3 * both
    heads = HEADS // 2
    per_head = half // heads
    start = pl.multiple_of(sample * nodes, nodes)
    first = lax.axis_index("dp") == 0
    queries = jnp.where(first, mine[pl.ds(start, nodes), :], came[pl.ds(start, nodes), :])
    keys = jnp.concatenate([pairs0[:, :half], keys1[...], pairs2[:, :half]], axis=0)
    values = jnp.concatenate([pairs0[:, half:], values1[...], pairs2[:, half:]], axis=0)
    times = times_ref[pl.ds(start, nodes), :][None]
    head_of = lax.broadcasted_iota(jnp.int32, (nodes, half), 1) // per_head
    zero = jnp.zeros_like(queries)
    stacked = jnp.concatenate(
        [jnp.where(head_of == h, queries, zero) for h in range(heads)], axis=0
    )
    logits = dot_nt(stacked, keys) * (1.0 / math.sqrt(per_head))
    logits = logits.reshape(heads, nodes, rows)
    logits = jnp.where(times > 0, logits, -1e30)
    top = jnp.max(logits, axis=-1, keepdims=True)
    weight = times * jnp.exp(logits - top)
    weight = weight / jnp.sum(weight, axis=-1, keepdims=True)
    mixed = dot(weight.astype(BF16).reshape(heads * nodes, rows), values)
    mixed = mixed.reshape(heads, nodes, half)
    total = jnp.where(head_of == 0, mixed[0], 0.0)
    for h in range(1, heads):
        total = jnp.where(head_of == h, mixed[h], total)
    return dot(total.astype(BF16), wo_ref[...])


def send_kernel(
    times_ref, mine, came, pairs0, keys1, values1, pairs2, wo_ref, send_ref
):
    other = 1 - lax.axis_index("dp")
    projected = mesh_attend(other, times_ref, mine, came, pairs0, keys1, values1, pairs2, wo_ref)
    send_ref[...] = projected.astype(BF16)


def keep_kernel(
    latent, limit, target, area, times_ref, mine, came, pairs0, keys1, values1, pairs2, wo_ref,
    keep_ref, weight_ref, base_ref,
):
    count_field, slots = target.shape
    valid = (lax.broadcasted_iota(jnp.int32, (8, slots), 1) < limit[...]).astype(F32)
    weight = valid * area[...]
    row = lax.broadcasted_iota(jnp.int32, (8, slots), 0)
    weight_ref[...] = jnp.where(row == 0, weight, valid)
    goal = target[...].astype(F32)
    squares = dot_nt(valid, goal * goal, lax.Precision.HIGHEST)
    here_count = jnp.broadcast_to(jnp.sum(valid, axis=1, keepdims=True), (8, count_field))
    here_weight = jnp.broadcast_to(jnp.sum(weight, axis=1, keepdims=True), (8, count_field))
    row = lax.broadcasted_iota(jnp.int32, (8, count_field), 0)
    base_ref[...] = jnp.where(row == 1, squares, jnp.where(row == 2, here_count, here_weight))
    ours = lax.axis_index("dp")
    nodes = keep_ref.shape[0]
    projected = mesh_attend(ours, times_ref, mine, came, pairs0, keys1, values1, pairs2, wo_ref)
    start = pl.multiple_of(ours * nodes, nodes)
    keep_ref[...] = latent[pl.ds(start, nodes), :].astype(F32) + projected


def decode_kernel(
    entries, counts, up0, left, right, up2, w1_ref, w2_ref, share,
    part_ref, rest_ref, hidden_ref, norm_ref,
):
    nodes = up0.shape[0]
    up1 = jnp.concatenate([left[...], right[...]], axis=1)
    mean = 0.0
    for i, updated in enumerate((up0[...], up1, up2[...])):
        mean += dot(counts[:, i * nodes : (i + 1) * nodes], updated)
    norm_ref[...] = normalize(mean * (1.0 / entries)).astype(BF16)
    hidden = silu(dot(norm_ref[...], w1_ref[...])).astype(BF16)
    part_ref[...] = dot_nt(w2_ref[...], hidden)
    size = hidden_ref.shape[1]
    core = lax.axis_index("space") % 2
    here = pl.multiple_of(core * size, size)
    there = pl.multiple_of((1 - core) * size, size)
    hidden_ref[...] = dot(norm_ref[:, pl.ds(here, size)], share[:size, :])
    rest_ref[...] = norm_ref[:, pl.ds(there, size)]


def errors_kernel(
    weight_ref, base_ref, fields, target, part_ref, rest_ref, hidden_ref, part0, part1,
    pred_ref, sums_ref, there_ref,
):
    count_field, slots = fields.shape
    core = lax.axis_index("space") % 2
    size = hidden_ref.shape[1]
    tail = part0.shape[0] - size
    for i, block in enumerate((part0, part1)):
        start = pl.multiple_of((core ^ i) * tail, tail)
        there_ref[pl.ds(start, tail), :] = block[size:, :]
    hidden = silu(hidden_ref[...] + dot(rest_ref[...], part1[:size, :])).astype(BF16)
    increment = part_ref[...] + dot_nt(there_ref[...], hidden)[:count_field]
    valid = weight_ref[1:2, :] > 0
    predicted = jnp.where(valid, fields[...].astype(F32) + increment, 0.0)
    pred_ref[...] = predicted.astype(BF16)
    misfit = predicted - target[...].astype(F32)
    errors = dot_nt(weight_ref[...], misfit * misfit, lax.Precision.HIGHEST)
    row = lax.broadcasted_iota(jnp.int32, (8, count_field), 0)
    sums = jnp.where(row == 0, errors, base_ref[...])
    sums_ref[...] = jnp.broadcast_to(sums[None], sums_ref.shape)


def loss_kernel(parts, loss_ref):
    total = jnp.sum(parts[...], axis=0)
    fields = total.shape[1]
    scaled = total[0:1] / (total[1:2] / total[2:3] + 1e-05)
    weight = total[3:4, 0:1]
    loss_ref[...] = jnp.sum(scaled, axis=1, keepdims=True) / (fields * weight)


def small_body(
    fields, target, area_weight, grid_count, mesh_query, enc_index, proc_index, dec_index,
    w_embed, w_enc_kv, w_qkv, w_out, w_dec1, w_dec2,
):
    space = lax.axis_size("space")
    samples = lax.axis_size("dp")
    own = fields[0].T
    goal = target[0].T
    w2 = w_dec2.T
    field_count, slots = own.shape
    nodes, width = mesh_query.shape
    half = width // 2
    rows = nodes * enc_index.shape[1]

    swap = [(0, 1), (1, 0)]
    pair = [(i, i ^ 1) for i in range(space)]
    link = [(i, i + 1) for i in range(1, space - 1, 2)]
    link = link + [(j, i) for i, j in link]

    def over_dp(x):
        return lax.ppermute(x, "dp", swap)

    def to_first(x):
        return lax.ppermute(x, "dp", swap)

    def to_second(x):
        return lax.ppermute(x, "dp", swap)

    def over_pair(x):
        return lax.ppermute(x, "space", pair)

    def over_link(x):
        return lax.ppermute(x, "space", link)

    def over_both(x, steps):
        steps = [(d * space + i, (1 - d) * space + j) for d in range(2) for i, j in steps]
        return lax.ppermute(x, ("dp", "space"), steps)

    def over_quad(x):
        return lax.ppermute(x, "space", [(i, i ^ 2) for i in range(space)])

    def after(x, *others):
        return lax.optimization_barrier((x,) + others)[0]

    we_there = over_dp(w_embed)
    own1 = over_pair(own)
    own2 = over_link(own)
    pick, present = call(
        pick_kernel,
        (shape((3, rows, slots)), shape((rows, 128), F32)),
        (enc_index.T,),
        flops=BUSY,
    )
    (near,) = call(
        near_kernel, (shape((field_count, rows)),), (pick, own, own1, own2), flops=BUSY
    )
    other = over_dp(near)
    tail = 16 * pl.cdiv(field_count, 128)
    share, times, counts = call(
        share_kernel,
        (
            shape((width // 8 + tail, half)),
            shape((2 * nodes, 6 * nodes), F32),
            shape((slots, 3 * nodes)),
        ),
        (proc_index.T, dec_index.T, after(w_dec1, near), w2),
        flops=BUSY,
    )
    pairs_own, probs = call(
        encode_own_kernel,
        (shape((rows, width)), shape((HEADS, rows))),
        (mesh_query, present, near, w_embed, we_there, w_enc_kv),
        flops=2 * rows * width * (width + field_count),
    )
    share = over_dp(after(share, other, pairs_own))
    pairs, probs = call(
        encode_other_kernel,
        (shape((rows, width)), shape((HEADS, 2 * rows))),
        (mesh_query, present, other, w_embed, we_there, w_enc_kv, probs),
        flops=2 * rows * width * (width + field_count),
    )
    (latent,) = call(
        latent_kernel,
        (shape((2 * nodes, width)),),
        (mesh_query, to_second(probs), pairs_own, pairs),
        flops=2 * 2 * rows * width * 128,
    )
    came = to_first(latent)
    share = after(share, latent)
    came_share = lax.ppermute(share, "space", [(i, i ^ 4) for i in range(space)])
    send, pairs = call(
        later_kernel,
        (shape((2 * nodes, half)), shape((2 * nodes, width))),
        (latent, w_qkv),
        flops=2 * 2 * nodes * width * 3 * half,
    )
    values = to_first(send)
    latent, queries, send, keys = call(
        first_kernel,
        (
            shape((2 * nodes, width)),
            shape((2 * nodes, half)),
            shape((2 * nodes + 16, half)),
            shape((2 * nodes, half)),
        ),
        (latent, came, w_qkv),
        flops=2 * 2 * nodes * width * 3 * half,
    )
    pairs, keys, values = call(
        pairs_kernel,
        (shape((2 * nodes, width)),) + (shape((2 * nodes, half)),) * 2,
        (pairs, keys, values),
    )
    (share,) = call(
        functools.partial(join_kernel, 4, tail),
        (shape((2 * share.shape[0], half)),),
        (share, came_share),
    )
    came_share = over_quad(share)
    window = (
        times, queries, to_second(send), pairs, over_pair(keys), over_pair(values),
        over_link(pairs), w_out,
    )
    (send,) = call(send_kernel, (shape((nodes, width)),), window, flops=4 * BUSY)
    keep, weight, base = call(
        keep_kernel,
        (shape((nodes, width), F32), shape((8, slots), F32), shape((8, field_count), F32)),
        (latent, grid_count[None], goal, area_weight[None]) + window,
        flops=2 * nodes * width * width,
    )
    (share,) = call(
        functools.partial(join_kernel, 2, 2 * tail),
        (shape((2 * share.shape[0], half)),),
        (share, came_share),
    )
    updated, left, right = call(
        add_kernel,
        (shape((nodes, width)),) + (shape((nodes, half)),) * 2,
        (keep, over_dp(send)),
    )
    left, right = over_pair(left), over_pair(right)
    up2 = over_link(updated)
    share = after(share, left, right, up2)
    came_share = over_pair(share)
    part, rest, hidden = call(
        functools.partial(decode_kernel, dec_index.shape[1]),
        (shape((field_count, slots), F32), shape((slots, half)), shape((slots, half), F32)),
        (counts, updated, left, right, up2, w_dec1, w2, share),
        scratch=[pltpu.VMEM((slots, width), BF16)],
        flops=2 * slots * width * half,
    )
    predicted, sums = call(
        errors_kernel,
        (shape((field_count, slots)), shape((space * samples, 8, field_count), F32)),
        (weight, base, own, goal, part, rest, hidden, share, came_share),
        scratch=[pltpu.VMEM((8 * tail, half), BF16)],
        flops=2 * slots * width * half,
    )
    parts = lax.all_to_all(sums, ("dp", "space"), 0, 0)
    (loss,) = call(loss_kernel, (shape((1, 1), F32),), (parts,))
    return predicted.T[None], loss[0, 0]


def with_halo(cells, sides, width):
    for axis, dim in sides:
        count = lax.axis_size(axis)
        ends = count - 1
        head = lax.slice_in_dim(cells, 0, width, axis=dim)
        tail = lax.slice_in_dim(cells, cells.shape[dim] - width, cells.shape[dim], axis=dim)
        cells = jnp.concatenate(
            [
                lax.ppermute(tail, axis, [(i, (i + 1) % count) for i in range(ends)]),
                cells,
                lax.ppermute(head, axis, [((i + 1) % count, i) for i in range(ends)]),
            ],
            axis=dim,
        )
    return cells


def layer_norm(values):
    centre = jnp.mean(values, axis=-1, keepdims=True)
    shifted = values - centre
    spread = jnp.mean(shifted * shifted, axis=-1, keepdims=True)
    return shifted / jnp.sqrt(spread + 1e-05)


def attend(queries, gathered, present):
    node_count, width = queries.shape
    per_head_width = width // HEADS
    split_query_heads = queries.reshape(node_count, HEADS, per_head_width)
    split_key_heads = gathered[:, :, :width].reshape(node_count, -1, HEADS, per_head_width)
    split_value_heads = gathered[:, :, width:].reshape(node_count, -1, HEADS, per_head_width)
    attention_logits = jnp.einsum(
        "gtz,gxtz->gtx", split_query_heads, split_key_heads, preferred_element_type=jnp.float32
    ) / math.sqrt(per_head_width)
    attention_logits = jnp.where(present[:, None, :], attention_logits, -jnp.inf)
    attention_probs = jax.nn.softmax(attention_logits, axis=-1).astype(jnp.bfloat16)
    aggregated_values = jnp.einsum(
        "owi,oiwn->own", attention_probs, split_value_heads, preferred_element_type=jnp.float32
    )
    return aggregated_values.reshape(node_count, width)


def general_body(
    fields,
    target,
    area_weight,
    grid_count,
    mesh_query,
    enc_index,
    proc_index,
    dec_index,
    w_embed,
    w_enc_kv,
    w_qkv,
    w_out,
    w_dec1,
    w_dec2,
):
    own_fields = fields[0]
    grid_rows = own_fields.shape[0]
    mesh_rows, width = mesh_query.shape
    field_count = own_fields.shape[1]
    grid_window = with_halo(
        jax.nn.silu(
            jnp.dot(
                own_fields,
                lax.all_gather(w_embed, "dp", axis=1, tiled=True),
                preferred_element_type=jnp.float32,
            )
        ).astype(jnp.bfloat16),
        (("space", 0),),
        grid_rows,
    )
    grid_pairs = jnp.dot(
        grid_window,
        lax.all_gather(w_enc_kv, "dp", axis=1, tiled=True),
        preferred_element_type=jnp.float32,
    ).astype(jnp.bfloat16)
    present = enc_index >= 0
    enc_near = jnp.take(grid_pairs, jnp.maximum(enc_index, 0), axis=0)
    latent = (mesh_query.astype(jnp.float32) + attend(mesh_query, enc_near, present)).astype(
        jnp.bfloat16
    )
    normed = layer_norm(latent.astype(jnp.float32)).astype(jnp.bfloat16)
    mesh_qkv = jnp.dot(
        normed, lax.all_gather(w_qkv, "dp", axis=1, tiled=True), preferred_element_type=jnp.float32
    ).astype(jnp.bfloat16)
    mesh_queries = mesh_qkv[:, :width]
    mesh_pairs = with_halo(mesh_qkv[:, width:], (("space", 0),), mesh_rows)
    proc_near = jnp.take(mesh_pairs, proc_index, axis=0)
    mixed = attend(mesh_queries, proc_near, jnp.ones(proc_index.shape, dtype=bool)).astype(
        jnp.bfloat16
    )
    columns = mixed
    projected = jnp.dot(
        columns, lax.all_gather(w_out, "dp", axis=0, tiled=True), preferred_element_type=jnp.float32
    )
    updated = (latent.astype(jnp.float32) + projected).astype(jnp.bfloat16)
    mesh_window = with_halo(updated, (("space", 0),), mesh_rows)
    dec_near = jnp.take(mesh_window, dec_index, axis=0).astype(jnp.float32)
    decoder_in = layer_norm(jnp.mean(dec_near, axis=1)).astype(jnp.bfloat16)
    decoder_hidden = jax.nn.silu(
        jnp.dot(
            decoder_in,
            lax.all_gather(w_dec1, "dp", axis=1, tiled=True),
            preferred_element_type=jnp.float32,
        )
    ).astype(jnp.bfloat16)
    columns = decoder_hidden
    increment = jnp.dot(
        columns,
        lax.all_gather(w_dec2, "dp", axis=0, tiled=True),
        preferred_element_type=jnp.float32,
    )
    valid = jnp.arange(grid_rows, dtype=jnp.int32) < grid_count[0]
    predicted = jnp.where(
        valid[:, None], own_fields.astype(jnp.float32) + increment, jnp.float32(0.0)
    )
    keep_mask = valid.astype(jnp.float32)
    target_rows = target[0].astype(jnp.float32)
    misfit = predicted - target_rows
    error_sums = jnp.sum((keep_mask * area_weight)[:, None] * misfit * misfit, axis=0)
    target_sums = jnp.sum(keep_mask[:, None] * target_rows * target_rows, axis=0)
    valid_count = jnp.sum(keep_mask)
    weight_sum = jnp.sum(keep_mask * area_weight)
    target_all, count_all, weight_all = lax.psum(
        (target_sums, valid_count, weight_sum), ("dp", "space")
    )
    local_loss = jnp.sum(error_sums / (target_all / count_all + 1e-05))
    loss = lax.psum(local_loss, ("dp", "space")) / (field_count * weight_all)
    return (predicted.astype(jnp.bfloat16)[None], loss)


def solution(mesh):
    placed = (
        P("dp", "space", None),
        P("dp", "space", None),
        P("space"),
        P("space"),
        P("space", None),
        P("space", None),
        P("space", None),
        P("space", None),
        P(None, "dp"),
        P(None, "dp"),
        P(None, "dp"),
        P("dp", None),
        P(None, "dp"),
        P("dp", None),
    )
    small = mesh.shape["dp"] == 2 and mesh.shape["space"] % 8 == 0
    return jax.shard_map(
        small_body if small else general_body, mesh=mesh, in_specs=placed, out_specs=(P("dp", "space", None), P()), check_vma=False
    )
```
